512 devices in a mesh: seq: 128 (over x, z, core), grp: 4 (over y).
Axes of the slice: x: 4, y: 4, z: 16, core: 2. Of those that a mesh axis runs over, the one named last changes fastest.
Arguments:
- queries: bfloat16 [65536, 512], P(('grp', 'seq')), may hold values from -32 to 32
- key_tokens: bfloat16 [65536, 512], P(('grp', 'seq')), may hold values from -20 to 20
- value_tokens: bfloat16 [65536, 512], P(('grp', 'seq')), may hold values from -12 to 12
- cotangent: bfloat16 [65536, 512], P(('grp', 'seq')), may hold values from -6 to 6
Outputs:
- attended: bfloat16 [65536, 512], P(('grp', 'seq'))
- query_grad: bfloat16 [65536, 512], P(('grp', 'seq'))
- key_grad: bfloat16 [65536, 512], P(('grp', 'seq'))
- value_grad: bfloat16 [65536, 512], P(('grp', 'seq'))
The draws below stay inside these ranges and needn't reach their ends.
All inputs are finite; a program needn't handle non-finite values.
Results may differ from the reference program's by a relative error of at most 0.04.
Values may be sent and summed in bfloat16 or wider, within the bound.
No kernel may reach another device: no remote copies, remote signals or barrier semaphores. Data moves between devices by JAX's collectives and lax.ppermute only.
A program may use at most 128 MiB of HBM per device.

```python
from functools import reduce
import jax
import jax.numpy as jnp
from jax import lax

HEADS = 8
HEAD_DIM = 64
BLOCK = 256
TOKENS = 65536
LEVELS = 8


def layered(key, base_scale, amount):
    feature_width = HEADS * HEAD_DIM
    noise_key = jax.random.fold_in(key, 1)
    noise = jax.random.normal(noise_key, (TOKENS, feature_width), jnp.float32)
    result = base_scale * noise
    for octave in range(2, 20, 2):
        coarse_rows = TOKENS >> octave
        if coarse_rows >= 2:
            coarse = jax.random.normal(jax.random.fold_in(key, 100 + octave), (coarse_rows, feature_width), jnp.float32)
            result = result + amount * jnp.repeat(coarse, 2 ** octave, axis=0)
    return result


def draw_queries(key, part):
    key = jax.random.fold_in(key, 11)
    result = layered(key, 0.5, 0.3)
    return jnp.clip(result, -32.0, 32.0).astype(jnp.bfloat16)


def draw_key_tokens(key, part):
    key = jax.random.fold_in(key, 12)
    result = layered(key, 0.5, 0.3)
    return jnp.clip(result, -20.0, 20.0).astype(jnp.bfloat16)


def draw_value_tokens(key, part):
    key = jax.random.fold_in(key, 13)
    result = layered(key, 0.7, 0.6)
    return jnp.clip(result, -12.0, 12.0).astype(jnp.bfloat16)


def block_levels(key, shape, split, least, largest):
    loudness, own = 1.0, jax.random.fold_in(key, 6)
    for dim, shards_of in split:
        heights = jnp.exp(jax.random.uniform(jax.random.fold_in(own, dim), (shards_of,), jnp.float32, least / len(split), largest / len(split)))
        loudness = loudness * jnp.repeat(heights, shape[dim] // shards_of).reshape([-1 if axis == dim else 1 for axis in range(len(shape))])
    return loudness


def gaussian(rng, extent, scale, most, cuts=(), kind=jnp.bfloat16):
    level = block_levels(rng, extent, cuts, -0.22, 0.18) if cuts else 1.0
    values = jax.random.normal(rng, extent, jnp.float32) * scale * level
    return jnp.minimum(jnp.maximum(values, -most), most).astype(kind)


def setup_inputs(seed: int = 0) -> dict:
    arg_keys = jax.random.split(jax.random.key(seed), 5)
    return {
        "queries": draw_queries(jax.random.fold_in(arg_keys[4], 71), 0),
        "key_tokens": draw_key_tokens(jax.random.fold_in(arg_keys[4], 71), 0),
        "value_tokens": draw_value_tokens(jax.random.fold_in(arg_keys[4], 71), 0),
        "cotangent": gaussian(arg_keys[3], (TOKENS, HEADS * HEAD_DIM), 1.0, 6.0, ((0, 512),)),
    }


def pool_pairs(matrix):
    half_rows = matrix.shape[0] // 2
    paired = matrix.reshape(half_rows, 2, matrix.shape[1]).astype(jnp.float32)
    return (0.5 * (paired[:, 0] + paired[:, 1])).astype(jnp.bfloat16)


def swap_halves(blocks):
    block_total = blocks.shape[0]
    paired = blocks.reshape((block_total // 2, 2) + blocks.shape[1:])
    return paired[:, ::-1].reshape(blocks.shape)


def hold_bf16(matrix):
    return lax.optimization_barrier(matrix.astype(jnp.bfloat16)).astype(jnp.float32)


def split_heads(matrix):
    return matrix.reshape(matrix.shape[:-1] + (HEADS, HEAD_DIM)).astype(jnp.float32)


def attend_blocks(query_blocks, key_blocks, value_blocks):
    query_heads = split_heads(query_blocks)
    key_heads = split_heads(key_blocks)
    value_heads = split_heads(value_blocks)
    scores = jnp.einsum("nrhd,nshd->nhrs", query_heads, key_heads) * (HEAD_DIM ** -0.5)
    highest = jnp.max(scores, axis=-1)
    weights = jnp.exp(scores - highest[..., None])
    totals = jnp.sum(weights, axis=-1)
    numerator = jnp.einsum("nhrs,nshd->nrhd", hold_bf16(weights), value_heads)
    return (jnp.swapaxes(highest, 1, 2), numerator.reshape(query_blocks.shape), jnp.swapaxes(totals, 1, 2))


def grad_blocks(query_blocks, key_blocks, value_blocks, floors, summed, products):
    query_heads = split_heads(query_blocks)
    key_heads = split_heads(key_blocks)
    value_heads = split_heads(value_blocks)
    summed_heads = split_heads(summed)
    scores = jnp.einsum("nrhd,nshd->nhrs", query_heads, key_heads) * (HEAD_DIM ** -0.5)
    shares = jnp.exp(scores - jnp.swapaxes(floors, 1, 2)[..., None])
    value_part = jnp.einsum("nhrs,nrhd->nshd", hold_bf16(shares), summed_heads)
    share_grad = jnp.einsum("nrhd,nshd->nhrs", summed_heads, value_heads)
    score_grad = hold_bf16(shares * (share_grad - jnp.swapaxes(products, 1, 2)[..., None]))
    query_part = jnp.einsum("nhrs,nshd->nrhd", score_grad, key_heads) * (HEAD_DIM ** -0.5)
    key_part = jnp.einsum("nhrs,nrhd->nshd", score_grad, query_heads) * (HEAD_DIM ** -0.5)
    return (query_part.reshape(query_blocks.shape), key_part.reshape(key_blocks.shape), value_part.reshape(value_blocks.shape))


def in_batches(function, arrays):
    block_total = arrays[0].shape[0]
    batch_rows = min(8, block_total)
    grouped = tuple(member.reshape((block_total // batch_rows, batch_rows) + member.shape[1:]) for member in arrays)
    result = lax.map(lambda group: function(*group), grouped)
    return tuple(outcome.reshape((block_total,) + outcome.shape[2:]) for outcome in result)


def level_blocks(level_arrays, height, feature_width):
    groups = TOKENS // (BLOCK << height)
    query_blocks = level_arrays[0][height].reshape(groups, BLOCK, feature_width)
    own_keys = level_arrays[1][height].reshape(groups, BLOCK, feature_width)
    own_values = level_arrays[2][height].reshape(groups, BLOCK, feature_width)
    key_blocks = swap_halves(own_keys)
    value_blocks = swap_halves(own_values)
    if height == 0:
        key_blocks = jnp.concatenate([own_keys, key_blocks], axis=1)
        value_blocks = jnp.concatenate([own_values, value_blocks], axis=1)
    return groups, query_blocks, key_blocks, value_blocks


def reference(queries, key_tokens, value_tokens, cotangent):
    feature_width = HEADS * HEAD_DIM
    query_levels = [queries]
    key_levels = [key_tokens]
    value_levels = [value_tokens]
    for height in range(1, LEVELS):
        query_levels.append(pool_pairs(query_levels[-1]))
        key_levels.append(pool_pairs(key_levels[-1]))
        value_levels.append(pool_pairs(value_levels[-1]))
    level_arrays = (query_levels, key_levels, value_levels)
    results = []
    for height in range(LEVELS):
        groups, query_blocks, key_blocks, value_blocks = level_blocks(level_arrays, height, feature_width)
        highest, numerator, totals = in_batches(attend_blocks, (query_blocks, key_blocks, value_blocks))
        coarse_rows = groups * BLOCK
        results.append((highest.reshape(coarse_rows, HEADS), numerator.reshape(coarse_rows, feature_width), totals.reshape(coarse_rows, HEADS)))
    peak = reduce(jnp.maximum, [jnp.repeat(results[height][0], 2 ** height, axis=0) for height in range(LEVELS)])
    accum = jnp.zeros((TOKENS, HEADS, HEAD_DIM), jnp.float32)
    denominator = jnp.zeros((TOKENS, HEADS), jnp.float32)
    for height in range(LEVELS):
        factor = 2 ** height
        weight = jnp.exp(jnp.repeat(results[height][0], factor, axis=0) - peak)
        accum = accum + weight[..., None] * jnp.repeat(results[height][1], factor, axis=0).reshape(TOKENS, HEADS, HEAD_DIM)
        denominator = denominator + weight * jnp.repeat(results[height][2], factor, axis=0)
    attended = (accum / denominator[..., None]).reshape(TOKENS, feature_width).astype(jnp.bfloat16)
    log_total = peak + jnp.log(denominator)
    drift = jnp.sum(split_heads(cotangent) * split_heads(attended), axis=-1)
    sums = None
    for height in reversed(range(LEVELS)):
        factor = 2 ** height
        coarse_rows = TOKENS // factor
        grouped = log_total.reshape(coarse_rows, factor, HEADS)
        floors = jnp.min(grouped, axis=1)
        scaling = jnp.exp(floors[:, None, :] - grouped)
        summed = jnp.sum(scaling[..., None] * split_heads(cotangent).reshape(coarse_rows, factor, HEADS, HEAD_DIM), axis=1)
        summed = summed.reshape(coarse_rows, feature_width).astype(jnp.bfloat16)
        products = jnp.sum(scaling * drift.reshape(coarse_rows, factor, HEADS), axis=1)
        groups, query_blocks, key_blocks, value_blocks = level_blocks(level_arrays, height, feature_width)
        query_part, key_part, value_part = in_batches(grad_blocks, (query_blocks, key_blocks, value_blocks, floors.reshape(groups, BLOCK, HEADS), summed.reshape(groups, BLOCK, feature_width), products.reshape(groups, BLOCK, HEADS)))
        if height == 0:
            key_part = key_part[:, :BLOCK] + swap_halves(key_part[:, BLOCK:])
            value_part = value_part[:, :BLOCK] + swap_halves(value_part[:, BLOCK:])
        else:
            key_part = swap_halves(key_part)
            value_part = swap_halves(value_part)
        parts = (query_part.reshape(coarse_rows, feature_width), key_part.reshape(coarse_rows, feature_width), value_part.reshape(coarse_rows, feature_width))
        if sums is None:
            sums = parts
        else:
            sums = tuple(0.5 * jnp.repeat(total, 2, axis=0) + part for total, part in zip(sums, parts))
    return (attended, sums[0].astype(jnp.bfloat16), sums[1].astype(jnp.bfloat16), sums[2].astype(jnp.bfloat16))
```

```python
import functools

import jax
import jax.numpy as jnp
from jax import lax
from jax.experimental import pallas as pl
from jax.experimental.pallas import tpu as pltpu
from jax.sharding import PartitionSpec as P

HEADS = 8
HEAD_DIM = 64
BLOCK = 256
LEVELS = 8
SHARD = 128
ROWS = HEADS * SHARD
LANES = 2 * HEAD_DIM
SCALE = HEAD_DIM**-0.5

SIZES = tuple(max(16, ROWS >> level) for level in range(LEVELS))
STARTS = tuple(sum(SIZES[:level]) for level in range(LEVELS))
TOTAL_ROWS = sum(SIZES)

VMEM = pl.BlockSpec(memory_space=pltpu.VMEM)
SMEM = pl.BlockSpec(memory_space=pltpu.SMEM)
F32 = jnp.float32
BF16 = jnp.bfloat16

NT = (((1,), (1,)), ((), ()))
NN = (((1,), (0,)), ((), ()))
TN = (((0,), (0,)), ((), ()))


def dot(left, right, dims):
    return lax.dot_general(left, right, dims, preferred_element_type=F32)


def shape(rows, kind, *lead):
    return jax.ShapeDtypeStruct(lead + rows, kind)


def low_lanes(rows):
    return lax.broadcasted_iota(jnp.int32, (rows, LANES), 1) < HEAD_DIM


def pool(values, scratch):
    rows = values.shape[0]
    scratch[0:rows, :] = values
    even = scratch[pl.ds(0, rows // 2, stride=2), :]
    odd = scratch[pl.ds(1, rows // 2, stride=2), :]
    return (0.5 * (even + odd)).astype(BF16).astype(F32)


def repeat_rows(values, times, scratch):
    rows = values.shape[0]
    for offset in range(times):
        scratch[pl.ds(offset, rows, stride=times), :] = values
    return scratch[0 : rows * times, :]


def pack_kernel(query_ref, key_ref, value_ref, cot_ref, out_ref):
    for head in range(HEADS):
        columns = slice(head * HEAD_DIM, (head + 1) * HEAD_DIM)
        out_ref[head, :, 0:LANES] = jnp.concatenate([cot_ref[:, columns], query_ref[:, columns]], axis=1)
        out_ref[head, :, LANES : 2 * LANES] = jnp.concatenate([value_ref[:, columns], key_ref[:, columns]], axis=1)


def unpack_kernel(in_ref, att_ref, query_ref, key_ref, value_ref):
    for pair in range(HEADS // 2):
        columns = slice(pair * LANES, (pair + 1) * LANES)
        left, right = in_ref[2 * pair], in_ref[2 * pair + 1]
        for place, target in enumerate((att_ref, query_ref, value_ref, key_ref)):
            part = slice(place * HEAD_DIM, (place + 1) * HEAD_DIM)
            target[:, columns] = jnp.concatenate([left[:, part], right[:, part]], axis=1)


def pool_own_kernel(own_ref, level1_ref, slots_ref, scratch):
    level1 = pool(own_ref[:, LANES : 2 * LANES].astype(F32), scratch)
    level1_ref[...] = level1.astype(BF16)
    level2 = pool(level1, scratch).astype(BF16)
    for place in range(4):
        slots_ref[place] = level2


def pool_region_kernel(region_ref, slots_ref, scratch):
    level3 = pool(region_ref[...].astype(F32), scratch)
    level4 = pool(level3, scratch).astype(BF16)
    for place in range(16):
        slots_ref[place] = level4


def main_kernel(
    place_ref, own_ref, level1_ref, near_ref, far_ref,
    front_ref, local_ref, grad2_ref, grad3_ref, send_ref,
    query_s, sum_s, weight_s, cross_s, upper_s, num_s, high_s, scaled_s, floor_s, sib_s, scr, scr2,
):
    near, far = place_ref[0], place_ref[1]

    def pooled_times(block, times):
        values = block.astype(F32)
        for _ in range(times):
            values = pool(values, scr2)
        return values.astype(BF16)

    sib_s[0] = near_ref[near ^ 1]
    for child in range(2):
        sib_s[1, 128 * child : 128 * (child + 1), :] = pooled_times(near_ref[((near ^ 2) & 2) + child], 1)
    sib_s[2] = far_ref[far ^ 1]
    for level in range(5, LEVELS):
        count = 2 ** (level - 4)
        base = (far ^ count) & (16 - count)
        part = BLOCK // count
        for child in range(count):
            sib_s[level - 2, part * child : part * (child + 1), :] = pooled_times(far_ref[base + child], level - 4)

    values = own_ref[:, 0:LANES].astype(F32)
    for level in range(LEVELS):
        rows = ROWS >> level
        kept = jnp.where(low_lanes(rows), 0.0, values * SCALE)
        if rows < SIZES[level]:
            kept = jnp.concatenate([kept, jnp.zeros((SIZES[level] - rows, LANES), F32)], axis=0)
        query_s[STARTS[level] : STARTS[level] + SIZES[level], :] = kept.astype(BF16)
        if level + 1 < LEVELS:
            values = pool(values, scr)

    tasks = []
    for half in range(2):
        keys = own_ref.at[512 * half : 512 * (half + 1), LANES : 2 * LANES]
        for piece in range(2):
            tasks.append((0, 512 * half + 256 * piece, 256, keys, weight_s.at[2 * half + piece], half))
    for half in range(2):
        keys = level1_ref.at[256 * (1 - half) : 256 * (2 - half), :]
        tasks.append((1, STARTS[1] + 256 * half, 256, keys, cross_s.at[half], half))
    for level in range(2, LEVELS):
        place = STARTS[level] - STARTS[2]
        kept = upper_s.at[place : place + SIZES[level], :]
        tasks.append((level, STARTS[level], SIZES[level], sib_s.at[level - 2], kept, 0))

    for level, first, rows, keys, kept, _ in tasks:
        key_rows = keys[...]
        scores = dot(query_s[first : first + rows, :], key_rows, NT)
        highest = jnp.max(scores, axis=1, keepdims=True)
        weights = jnp.exp(scores - highest).astype(BF16)
        kept[...] = weights
        ones = jnp.ones((key_rows.shape[0], LANES), BF16)
        num_s[first : first + rows, :] = dot(weights, jnp.where(low_lanes(key_rows.shape[0]), key_rows, ones), NN)
        high_s[first : first + rows, :] = jnp.broadcast_to(highest, (rows, LANES))

    rows = ROWS >> (LEVELS - 1)
    peak = high_s[STARTS[-1] : STARTS[-1] + rows, :]
    accum = num_s[STARTS[-1] : STARTS[-1] + rows, :]
    for level in reversed(range(1, LEVELS - 1)):
        peak_up = repeat_rows(peak, 2, scr)
        accum_up = repeat_rows(accum, 2, scr2)
        rows = ROWS >> level
        high = high_s[STARTS[level] : STARTS[level] + rows, :]
        num = num_s[STARTS[level] : STARTS[level] + rows, :]
        peak = jnp.maximum(peak_up, high)
        accum = jnp.exp(peak_up - peak) * accum_up + jnp.exp(high - peak) * num
    repeat_rows(peak, 2, scr)
    repeat_rows(accum, 2, scr2)
    chunk = 128
    low = low_lanes(chunk)
    for first in range(0, ROWS, chunk):
        span = slice(first, first + chunk)
        peak_up, high = scr[span, :], high_s[span, :]
        peak = jnp.maximum(peak_up, high)
        accum = jnp.exp(peak_up - peak) * scr2[span, :] + jnp.exp(high - peak) * num_s[span, :]
        total = jnp.where(low, pltpu.roll(accum, HEAD_DIM, 1), accum)
        attended = (accum / total).astype(BF16)
        front_ref[span, :] = attended
        cot = own_ref[span, 0:LANES].astype(F32)
        drift = jnp.sum(jnp.where(low, cot * attended.astype(F32), 0.0), axis=1, keepdims=True)
        floor_s[span, :] = peak + jnp.log(total)
        scaled_s[span, :] = jnp.where(low, cot, drift)

    for level in range(LEVELS - 1):
        start, rows = STARTS[level], ROWS >> (level + 1)
        even, odd = pl.ds(start, rows, stride=2), pl.ds(start + 1, rows, stride=2)
        floor = jnp.minimum(floor_s[even, :], floor_s[odd, :])
        scaled = jnp.exp(floor - floor_s[even, :]) * scaled_s[even, :] + jnp.exp(floor - floor_s[odd, :]) * scaled_s[odd, :]
        target = slice(STARTS[level + 1], STARTS[level + 1] + rows)
        floor_s[target, :] = floor
        scaled_s[target, :] = scaled
    for level in range(LEVELS):
        start, rows = STARTS[level], ROWS >> level
        for first in range(start, start + rows, 256):
            span = slice(first, first + min(rows, 256))
            scaled = jnp.exp(high_s[span, :] - floor_s[span, :]) * scaled_s[span, :]
            scaled_s[span, :] = scaled
        if rows < SIZES[level]:
            scaled_s[start + rows : start + SIZES[level], :] = jnp.zeros((SIZES[level] - rows, LANES), F32)
    for first in range(0, TOTAL_ROWS, 256):
        span = slice(first, first + 256)
        sum_s[span, :] = jnp.where(low_lanes(256), scaled_s[span, :], 0.0).astype(BF16)

    def gradients(task):
        level, first, rows, keys, kept, _ = task
        span = slice(first, first + rows)
        key_rows = keys[...]
        sums, queries, weights = sum_s[span, :], query_s[span, :], kept[...]
        share_grad = dot(sums, key_rows, NT)
        score_grad = (weights.astype(F32) * (share_grad - scaled_s[span, HEAD_DIM : HEAD_DIM + 1])).astype(BF16)
        query_part = dot(score_grad, key_rows, NN)
        key_part = dot(queries, score_grad, TN) + dot(sums, weights, TN)
        return query_part, key_part

    query_sum = None
    for task in reversed(tasks[6:]):
        query_part, key_part = gradients(task)
        level = task[0]
        rows = ROWS >> level
        query_part = query_part[0:rows, :]
        if query_sum is not None:
            query_part = query_part + 0.5 * repeat_rows(query_sum, 2, scr)
        query_sum = query_part
        key_part = key_part.T
        if level >= 4:
            count = 2 ** (level - 4)
            base = (far ^ count) & (16 - count)
            part = BLOCK // count
            for child in range(count):
                send_ref[base + child, 0:part, :] = key_part[part * child : part * (child + 1), :].astype(BF16)
        elif level == 3:
            grad3_ref[...] = key_part
        else:
            grad2_ref[...] = key_part
    send_ref[far] = jnp.zeros((BLOCK, LANES), BF16)

    cross_grads = [gradients(task) for task in tasks[4:6]]
    query_sum = 0.5 * repeat_rows(query_sum, 2, scr) + jnp.concatenate([part[0] for part in cross_grads], axis=0)
    repeat_rows(query_sum, 2, scr)
    repeat_rows(jnp.concatenate([cross_grads[1][1].T, cross_grads[0][1].T], axis=0), 2, scr2)
    for half in range(2):
        total = None
        for task in tasks[2 * half : 2 * half + 2]:
            query_part, key_part = gradients(task)
            span = slice(task[1], task[1] + 256)
            query_part = SCALE * (query_part + 0.5 * scr[span, :])
            front_ref[span, :] = jnp.where(low_lanes(256), front_ref[span, :], query_part.astype(BF16))
            total = key_part if total is None else total + key_part
        span = slice(512 * half, 512 * (half + 1))
        local_ref[span, :] = total.T + 0.5 * scr2[span, :]


def near_grads_kernel(place_ref, got_ref, grad2_ref, grad3_ref, slots_ref, sums, scr):
    near, far = place_ref[0], place_ref[1]
    total = None
    for level in reversed(range(4, LEVELS)):
        count = 2 ** (level - 4)
        base = (far ^ count) & (16 - count)
        part = BLOCK // count
        here = got_ref[base, 0:part, :].astype(F32)
        for child in range(1, count):
            here = here + got_ref[base + child, 0:part, :].astype(F32)
        total = here if total is None else here + 0.5 * repeat_rows(total, 2, scr)
    for place in range(4):
        sums[place] = 0.25 * repeat_rows(total[64 * place : 64 * (place + 1), :], 4, scr)
    sums[near ^ 1] = sums[near ^ 1] + grad2_ref[...]
    for child in range(2):
        place = ((near ^ 2) & 2) + child
        sums[place] = sums[place] + 0.5 * repeat_rows(grad3_ref[128 * child : 128 * (child + 1), :], 2, scr)
    for place in range(4):
        slots_ref[place] = sums[place].astype(BF16)


def own_grads_kernel(got_ref, local_ref, front_ref, out_ref, scr):
    total = got_ref[0].astype(F32)
    for place in range(1, 4):
        total = total + got_ref[place].astype(F32)
    repeat_rows(total, 4, scr)
    for head in range(HEADS):
        span = slice(head * SHARD, (head + 1) * SHARD)
        out_ref[head, :, 0:LANES] = front_ref[span, :]
        out_ref[head, :, LANES : 2 * LANES] = (local_ref[span, :] + 0.25 * scr[span, :]).astype(BF16)


def call(kernel, outs, scratch, megabytes, in_specs):
    return pl.pallas_call(
        kernel,
        out_shape=outs,
        in_specs=in_specs,
        out_specs=jax.tree.map(lambda _: VMEM, outs),
        scratch_shapes=scratch,
        compiler_params=pltpu.CompilerParams(vmem_limit_bytes=megabytes * 2**20),
    )


def wide(rows):
    return pltpu.VMEM((rows, LANES), F32)


def on_device(near_groups, far_groups, head_groups, queries, key_tokens, value_tokens, cotangent):
    seq_place, grp_place = lax.axis_index("seq"), lax.axis_index("grp")
    place = jnp.stack([seq_place >> 3 & 3, (seq_place >> 5 & 3) | grp_place << 2]).astype(jnp.int32)

    def exchange(slots, groups):
        return lax.all_to_all(slots, ("grp", "seq"), 0, 0, axis_index_groups=groups)

    packed = call(pack_kernel, shape((HEADS, SHARD, 2 * LANES), BF16), [], 8, [VMEM] * 4)(
        queries, key_tokens, value_tokens, cotangent
    )
    own = exchange(packed, head_groups).reshape(ROWS, 2 * LANES)
    level1, slots = call(
        pool_own_kernel,
        (shape((512, LANES), BF16), shape((4, BLOCK, LANES), BF16)),
        [wide(ROWS)], 8, [VMEM],
    )(own)
    near_rows = exchange(slots, near_groups)
    slots = call(pool_region_kernel, shape((16, BLOCK, LANES), BF16), [wide(ROWS)], 8, [VMEM])(
        near_rows.reshape(ROWS, LANES)
    )
    far_rows = exchange(slots, far_groups)
    upper_rows = TOTAL_ROWS - STARTS[2]
    front, local, grad2, grad3, slots = call(
        main_kernel,
        (
            shape((ROWS, LANES), BF16),
            shape((ROWS, LANES), F32),
            shape((BLOCK, LANES), F32),
            shape((BLOCK, LANES), F32),
            shape((16, BLOCK, LANES), BF16),
        ),
        [
            pltpu.VMEM((TOTAL_ROWS, LANES), BF16),
            pltpu.VMEM((TOTAL_ROWS, LANES), BF16),
            pltpu.VMEM((4, 256, 512), BF16),
            pltpu.VMEM((2, 256, 256), BF16),
            pltpu.VMEM((upper_rows, 256), BF16),
            wide(TOTAL_ROWS),
            wide(TOTAL_ROWS),
            wide(TOTAL_ROWS),
            wide(TOTAL_ROWS),
            pltpu.VMEM((6, BLOCK, LANES), BF16),
            wide(ROWS),
            wide(ROWS),
        ],
        32,
        [SMEM] + [VMEM] * 4,
    )(place, own, level1, near_rows, far_rows)
    slots = call(
        near_grads_kernel,
        shape((4, BLOCK, LANES), BF16),
        [pltpu.VMEM((4, BLOCK, LANES), F32), wide(BLOCK)],
        8, [SMEM] + [VMEM] * 3,
    )(place, exchange(slots, far_groups), grad2, grad3)
    packed = call(own_grads_kernel, shape((HEADS, SHARD, 2 * LANES), BF16), [wide(ROWS)], 8, [VMEM] * 3)(
        exchange(slots, near_groups), local, front
    )
    return call(unpack_kernel, (shape((SHARD, HEADS * HEAD_DIM), BF16),) * 4, [], 8, [VMEM])(
        exchange(packed, head_groups)
    )


def groups_over(bits, devices):
    mask = sum(1 << bit for bit in bits)
    offsets = [sum((number >> order & 1) << bit for order, bit in enumerate(bits)) for number in range(2 ** len(bits))]
    return [[base + offset for offset in offsets] for base in range(devices) if base & mask == 0]


def solution(mesh):
    devices = mesh.size
    spec = P(("grp", "seq"), None)
    return jax.shard_map(
        functools.partial(
            on_device,
            groups_over((3, 4), devices),
            groups_over((5, 6, 7, 8), devices),
            groups_over((0, 1, 2), devices),
        ),
        mesh=mesh,
        in_specs=(spec,) * 4,
        out_specs=(spec,) * 4,
        check_vma=False,
    )
```

```python
import functools

import jax
import jax.numpy as jnp
from jax import lax
from jax.experimental import pallas as pl
from jax.experimental.pallas import tpu as pltpu
from jax.sharding import PartitionSpec as P

HEADS = 8
HEAD_DIM = 64
BLOCK = 256
LEVELS = 8
SHARD = 128
ROWS = HEADS * SHARD
LANES = 2 * HEAD_DIM
SCALE = HEAD_DIM**-0.5

SIZES = tuple(max(16, ROWS >> level) for level in range(LEVELS))
STARTS = tuple(sum(SIZES[:level]) for level in range(LEVELS))
TOTAL_ROWS = sum(SIZES)

VMEM = pl.BlockSpec(memory_space=pltpu.VMEM)
SMEM = pl.BlockSpec(memory_space=pltpu.SMEM)
F32 = jnp.float32
BF16 = jnp.bfloat16

NT = (((1,), (1,)), ((), ()))
NN = (((1,), (0,)), ((), ()))
TN = (((0,), (0,)), ((), ()))


def dot(left, right, dims):
    return lax.dot_general(left, right, dims, preferred_element_type=F32)


def shape(rows, kind, *lead):
    return jax.ShapeDtypeStruct(lead + rows, kind)


def low_lanes(rows):
    return lax.broadcasted_iota(jnp.int32, (rows, LANES), 1) < HEAD_DIM


def pool(values, scratch):
    rows = values.shape[0]
    scratch[0:rows, :] = values
    even = scratch[pl.ds(0, rows // 2, stride=2), :]
    odd = scratch[pl.ds(1, rows // 2, stride=2), :]
    return (0.5 * (even + odd)).astype(BF16).astype(F32)


def repeat_rows(values, times, scratch):
    rows = values.shape[0]
    for offset in range(times):
        scratch[pl.ds(offset, rows, stride=times), :] = values
    return scratch[0 : rows * times, :]


def pack_kernel(query_hbm, key_hbm, value_hbm, cot_hbm, out_ref, query_ref, key_ref, value_ref, cot_ref, sems):
    sources = (cot_hbm, query_hbm, value_hbm, key_hbm)
    targets = (cot_ref, query_ref, value_ref, key_ref)
    copies = [pltpu.make_async_copy(source, target, sems.at[n]) for n, (source, target) in enumerate(zip(sources, targets))]
    for copy in copies:
        copy.start()
    for side in range(2):
        copies[2 * side].wait()
        copies[2 * side + 1].wait()
        left, right = targets[2 * side], targets[2 * side + 1]
        for head in range(HEADS):
            columns = slice(head * HEAD_DIM, (head + 1) * HEAD_DIM)
            rows = jnp.concatenate([left[:, columns], right[:, columns]], axis=1)
            out_ref[head, :, LANES * side : LANES * (side + 1)] = rows


def unpack_kernel(in_ref, att_ref, query_ref, key_ref, value_ref):
    for pair in range(HEADS // 2):
        columns = slice(pair * LANES, (pair + 1) * LANES)
        left, right = in_ref[2 * pair], in_ref[2 * pair + 1]
        for place, target in enumerate((att_ref, query_ref, value_ref, key_ref)):
            part = slice(place * HEAD_DIM, (place + 1) * HEAD_DIM)
            target[:, columns] = jnp.concatenate([left[:, part], right[:, part]], axis=1)


def pool_own_kernel(own_ref, level1_ref, level2_ref, scratch):
    level1 = pool(own_ref[:, LANES : 2 * LANES].astype(F32), scratch)
    level1_ref[...] = level1.astype(BF16)
    level2_ref[...] = pool(level1, scratch).astype(BF16)


def join_pooled(side, own_ref, sibling_ref, scratch):
    own = pool(own_ref[...].astype(F32), scratch)
    sibling = pool(sibling_ref[...].astype(F32), scratch)
    upper = side == 1
    return jnp.concatenate([jnp.where(upper, sibling, own), jnp.where(upper, own, sibling)], axis=0)


def climb_kernel(place_ref, own_ref, sibling_ref, out_ref, scratch):
    out_ref[...] = join_pooled(place_ref[0], own_ref, sibling_ref, scratch).astype(BF16)


def climb_last_kernel(place_ref, own_ref, sibling_ref, out_ref, slots_ref, scratch):
    joined = join_pooled(place_ref[1], own_ref, sibling_ref, scratch)
    out_ref[...] = joined.astype(BF16)
    pooled = pool(joined, scratch).astype(BF16)
    for place in range(16):
        slots_ref[place] = pooled


def main_kernel(
    place_ref, own_ref, level1_ref, sib2_ref, sib3_ref, sib4_ref, far_ref,
    front_ref, local_ref, grad2_ref, grad3_ref, grad4_ref, send_ref,
    query_s, sum_s, weight_s, cross_s, upper_s, num_s, high_s, scaled_s, floor_s, sib_s, scr, scr2,
):
    far = place_ref[2]

    def pooled_times(block, times):
        values = block.astype(F32)
        for _ in range(times):
            values = pool(values, scr2)
        return values.astype(BF16)

    for level in range(5, LEVELS):
        count = 2 ** (level - 4)
        base = (far ^ count) & (16 - count)
        part = BLOCK // count
        for child in range(count):
            sib_s[level - 5, part * child : part * (child + 1), :] = pooled_times(far_ref[base + child], level - 5)
    siblings = [sib2_ref, sib3_ref, sib4_ref] + [sib_s.at[number] for number in range(3)]

    values = own_ref[:, 0:LANES].astype(F32)
    for level in range(LEVELS):
        rows = ROWS >> level
        kept = jnp.where(low_lanes(rows), 0.0, values * SCALE)
        if rows < SIZES[level]:
            kept = jnp.concatenate([kept, jnp.zeros((SIZES[level] - rows, LANES), F32)], axis=0)
        query_s[STARTS[level] : STARTS[level] + SIZES[level], :] = kept.astype(BF16)
        if level + 1 < LEVELS:
            values = pool(values, scr)

    tasks = []
    for half in range(2):
        keys = own_ref.at[512 * half : 512 * (half + 1), LANES : 2 * LANES]
        for piece in range(2):
            tasks.append((0, 512 * half + 256 * piece, 256, keys, weight_s.at[2 * half + piece], half))
    for half in range(2):
        keys = level1_ref.at[256 * (1 - half) : 256 * (2 - half), :]
        tasks.append((1, STARTS[1] + 256 * half, 256, keys, cross_s.at[half], half))
    for level in range(2, LEVELS):
        place = STARTS[level] - STARTS[2]
        kept = upper_s.at[place : place + SIZES[level], :]
        tasks.append((level, STARTS[level], SIZES[level], siblings[level - 2], kept, 0))

    for level, first, rows, keys, kept, _ in tasks:
        key_rows = keys[...]
        scores = dot(query_s[first : first + rows, :], key_rows, NT)
        highest = jnp.max(scores, axis=1, keepdims=True)
        weights = jnp.exp(scores - highest).astype(BF16)
        kept[...] = weights
        ones = jnp.ones((key_rows.shape[0], LANES), BF16)
        num_s[first : first + rows, :] = dot(weights, jnp.where(low_lanes(key_rows.shape[0]), key_rows, ones), NN)
        high_s[first : first + rows, :] = jnp.broadcast_to(highest, (rows, LANES))

    rows = ROWS >> (LEVELS - 1)
    peak = high_s[STARTS[-1] : STARTS[-1] + rows, :]
    accum = num_s[STARTS[-1] : STARTS[-1] + rows, :]
    for level in reversed(range(1, LEVELS - 1)):
        peak_up = repeat_rows(peak, 2, scr)
        accum_up = repeat_rows(accum, 2, scr2)
        rows = ROWS >> level
        high = high_s[STARTS[level] : STARTS[level] + rows, :]
        num = num_s[STARTS[level] : STARTS[level] + rows, :]
        peak = jnp.maximum(peak_up, high)
        accum = jnp.exp(peak_up - peak) * accum_up + jnp.exp(high - peak) * num
    repeat_rows(peak, 2, scr)
    repeat_rows(accum, 2, scr2)
    chunk = 128
    low = low_lanes(chunk)
    for first in range(0, ROWS, chunk):
        span = slice(first, first + chunk)
        peak_up, high = scr[span, :], high_s[span, :]
        peak = jnp.maximum(peak_up, high)
        accum = jnp.exp(peak_up - peak) * scr2[span, :] + jnp.exp(high - peak) * num_s[span, :]
        total = jnp.where(low, pltpu.roll(accum, HEAD_DIM, 1), accum)
        attended = (accum / total).astype(BF16)
        front_ref[span, :] = attended
        cot = own_ref[span, 0:LANES].astype(F32)
        drift = jnp.sum(jnp.where(low, cot * attended.astype(F32), 0.0), axis=1, keepdims=True)
        floor_s[span, :] = peak + jnp.log(total)
        scaled_s[span, :] = jnp.where(low, cot, drift)

    for level in range(LEVELS - 1):
        start, rows = STARTS[level], ROWS >> (level + 1)
        even, odd = pl.ds(start, rows, stride=2), pl.ds(start + 1, rows, stride=2)
        floor = jnp.minimum(floor_s[even, :], floor_s[odd, :])
        scaled = jnp.exp(floor - floor_s[even, :]) * scaled_s[even, :] + jnp.exp(floor - floor_s[odd, :]) * scaled_s[odd, :]
        target = slice(STARTS[level + 1], STARTS[level + 1] + rows)
        floor_s[target, :] = floor
        scaled_s[target, :] = scaled
    for level in range(LEVELS):
        start, rows = STARTS[level], ROWS >> level
        for first in range(start, start + rows, 256):
            span = slice(first, first + min(rows, 256))
            scaled = jnp.exp(high_s[span, :] - floor_s[span, :]) * scaled_s[span, :]
            scaled_s[span, :] = scaled
        if rows < SIZES[level]:
            scaled_s[start + rows : start + SIZES[level], :] = jnp.zeros((SIZES[level] - rows, LANES), F32)
    for first in range(0, TOTAL_ROWS, 256):
        span = slice(first, first + 256)
        sum_s[span, :] = jnp.where(low_lanes(256), scaled_s[span, :], 0.0).astype(BF16)

    def gradients(task):
        level, first, rows, keys, kept, _ = task
        span = slice(first, first + rows)
        key_rows = keys[...]
        sums, queries, weights = sum_s[span, :], query_s[span, :], kept[...]
        share_grad = dot(sums, key_rows, NT)
        score_grad = (weights.astype(F32) * (share_grad - scaled_s[span, HEAD_DIM : HEAD_DIM + 1])).astype(BF16)
        query_part = dot(score_grad, key_rows, NN)
        key_part = dot(queries, score_grad, TN) + dot(sums, weights, TN)
        return query_part, key_part

    query_sum = None
    for task in reversed(tasks[6:]):
        query_part, key_part = gradients(task)
        level = task[0]
        rows = ROWS >> level
        query_part = query_part[0:rows, :]
        if query_sum is not None:
            query_part = query_part + 0.5 * repeat_rows(query_sum, 2, scr)
        query_sum = query_part
        key_part = key_part.T
        if level >= 5:
            count = 2 ** (level - 4)
            base = (far ^ count) & (16 - count)
            part = BLOCK // count
            for child in range(count):
                send_ref[base + child, 0:part, :] = key_part[part * child : part * (child + 1), :].astype(BF16)
        elif level == 4:
            grad4_ref[...] = key_part.astype(BF16)
        elif level == 3:
            grad3_ref[...] = key_part
        else:
            grad2_ref[...] = key_part
    send_ref[far] = jnp.zeros((SHARD, LANES), BF16)
    send_ref[far ^ 1] = jnp.zeros((SHARD, LANES), BF16)

    cross_grads = [gradients(task) for task in tasks[4:6]]
    query_sum = 0.5 * repeat_rows(query_sum, 2, scr) + jnp.concatenate([part[0] for part in cross_grads], axis=0)
    repeat_rows(query_sum, 2, scr)
    repeat_rows(jnp.concatenate([cross_grads[1][1].T, cross_grads[0][1].T], axis=0), 2, scr2)
    for half in range(2):
        total = None
        for task in tasks[2 * half : 2 * half + 2]:
            query_part, key_part = gradients(task)
            span = slice(task[1], task[1] + 256)
            query_part = SCALE * (query_part + 0.5 * scr[span, :])
            front_ref[span, :] = jnp.where(low_lanes(256), front_ref[span, :], query_part.astype(BF16))
            total = key_part if total is None else total + key_part
        span = slice(512 * half, 512 * (half + 1))
        local_ref[span, :] = total.T + 0.5 * scr2[span, :]


def far_grads_kernel(place_ref, got_ref, got4_ref, grad3_ref, keep_ref, out_ref, sums, scr):
    side, far = place_ref[1], place_ref[2]
    total = None
    for level in reversed(range(5, LEVELS)):
        count = 2 ** (level - 4)
        base = (far ^ count) & (16 - count)
        part = BLOCK // count
        here = got_ref[base, 0:part, :].astype(F32)
        for child in range(1, count):
            here = here + got_ref[base + child, 0:part, :].astype(F32)
        total = here if total is None else here + 0.5 * repeat_rows(total, 2, scr)
    total = got4_ref[...].astype(F32) + 0.5 * repeat_rows(total, 2, scr)
    sums[...] = total.reshape(2, SHARD, LANES)
    keep_ref[...] = 0.5 * repeat_rows(sums[side], 2, scr)
    out_ref[...] = (grad3_ref[...] + 0.5 * repeat_rows(sums[1 - side], 2, scr)).astype(BF16)


def near_grads_kernel(place_ref, got_ref, kept_ref, grad2_ref, keep_ref, out_ref, sums, scr):
    side = place_ref[0]
    sums[...] = (kept_ref[...] + got_ref[...].astype(F32)).reshape(2, SHARD, LANES)
    keep_ref[...] = 0.5 * repeat_rows(sums[side], 2, scr)
    out_ref[...] = (grad2_ref[...] + 0.5 * repeat_rows(sums[1 - side], 2, scr)).astype(BF16)


def own_grads_kernel(got_ref, kept_ref, local_ref, front_ref, out_ref, scr):
    repeat_rows(kept_ref[...] + got_ref[...].astype(F32), 4, scr)
    for head in range(HEADS):
        span = slice(head * SHARD, (head + 1) * SHARD)
        out_ref[head, :, 0:LANES] = front_ref[span, :]
        out_ref[head, :, LANES : 2 * LANES] = (local_ref[span, :] + 0.25 * scr[span, :]).astype(BF16)


def call(kernel, outs, scratch, megabytes, in_specs):
    return pl.pallas_call(
        kernel,
        out_shape=outs,
        in_specs=in_specs,
        out_specs=jax.tree.map(lambda _: VMEM, outs),
        scratch_shapes=scratch,
        compiler_params=pltpu.CompilerParams(vmem_limit_bytes=megabytes * 2**20),
    )


def wide(rows):
    return pltpu.VMEM((rows, LANES), F32)


def on_device(far_groups, head_groups, queries, key_tokens, value_tokens, cotangent):
    seq_place, grp_place = lax.axis_index("seq"), lax.axis_index("grp")
    far_place = (seq_place >> 5 & 3) | grp_place << 2
    place = jnp.stack([seq_place >> 3 & 1, seq_place >> 4 & 1, far_place]).astype(jnp.int32)
    block, block32 = shape((BLOCK, LANES), BF16), shape((BLOCK, LANES), F32)
    packed_shape = shape((HEADS, SHARD, 2 * LANES), BF16)

    def exchange(slots, groups):
        return lax.all_to_all(slots, ("grp", "seq"), 0, 0, axis_index_groups=groups)

    def swap(rows, mask):
        return lax.ppermute(rows, "seq", [(source, source ^ mask) for source in range(lax.axis_size("seq"))])

    packed = call(
        pack_kernel,
        packed_shape,
        [pltpu.VMEM((SHARD, HEADS * HEAD_DIM), BF16)] * 4 + [pltpu.SemaphoreType.DMA((4,))],
        60,
        [pl.BlockSpec(memory_space=pl.ANY)] * 4,
    )(queries, key_tokens, value_tokens, cotangent)
    own = exchange(packed, head_groups).reshape(ROWS, 2 * LANES)
    level1, level2 = call(pool_own_kernel, (shape((512, LANES), BF16), block), [wide(ROWS)], 8, [VMEM])(own)
    sib2 = swap(level2, 8)
    level3 = call(climb_kernel, block, [wide(BLOCK)], 8, [SMEM, VMEM, VMEM])(place, level2, sib2)
    sib3 = swap(level3, 24)
    level4, slots = call(
        climb_last_kernel, (block, shape((16, SHARD, LANES), BF16)), [wide(BLOCK)], 8, [SMEM, VMEM, VMEM]
    )(place, level3, sib3)
    sib4 = swap(level4, 32)
    far_rows = exchange(slots, far_groups)
    upper_rows = TOTAL_ROWS - STARTS[2]
    front, local, grad2, grad3, grad4, slots = call(
        main_kernel,
        (
            shape((ROWS, LANES), BF16),
            shape((ROWS, LANES), F32),
            block32,
            block32,
            block,
            shape((16, SHARD, LANES), BF16),
        ),
        [
            pltpu.VMEM((TOTAL_ROWS, LANES), BF16),
            pltpu.VMEM((TOTAL_ROWS, LANES), BF16),
            pltpu.VMEM((4, 256, 512), BF16),
            pltpu.VMEM((2, 256, 256), BF16),
            pltpu.VMEM((upper_rows, 256), BF16),
            wide(TOTAL_ROWS),
            wide(TOTAL_ROWS),
            wide(TOTAL_ROWS),
            wide(TOTAL_ROWS),
            pltpu.VMEM((3, BLOCK, LANES), BF16),
            wide(ROWS),
            wide(ROWS),
        ],
        32,
        [SMEM] + [VMEM] * 6,
    )(place, own, level1, sib2, sib3, sib4, far_rows)
    scratch = [pltpu.VMEM((2, SHARD, LANES), F32), wide(BLOCK)]
    got4 = swap(grad4, 32)
    kept, rows = call(far_grads_kernel, (block32, block), scratch, 8, [SMEM] + [VMEM] * 3)(
        place, exchange(slots, far_groups), got4, grad3
    )
    kept, rows = call(near_grads_kernel, (block32, block), scratch, 8, [SMEM] + [VMEM] * 3)(
        place, swap(rows, 24), kept, grad2
    )
    packed = call(own_grads_kernel, packed_shape, [wide(ROWS)], 8, [VMEM] * 4)(swap(rows, 8), kept, local, front)
    return call(unpack_kernel, (shape((SHARD, HEADS * HEAD_DIM), BF16),) * 4, [], 8, [VMEM])(
        exchange(packed, head_groups)
    )


def groups_over(bits, devices):
    mask = sum(1 << bit for bit in bits)
    offsets = [sum((number >> order & 1) << bit for order, bit in enumerate(bits)) for number in range(2 ** len(bits))]
    return [[base + offset for offset in offsets] for base in range(devices) if base & mask == 0]


def solution(mesh):
    devices = mesh.size
    spec = P(("grp", "seq"), None)
    return jax.shard_map(
        functools.partial(
            on_device,
            groups_over((5, 6, 7, 8), devices),
            groups_over((0, 1, 2), devices),
        ),
        mesh=mesh,
        in_specs=(spec,) * 4,
        out_specs=(spec,) * 4,
        check_vma=False,
    )
```

```python
import functools

import jax
import jax.numpy as jnp
from jax import lax
from jax.experimental import pallas as pl
from jax.experimental.pallas import tpu as pltpu
from jax.sharding import PartitionSpec as P

HEADS = 8
HEAD_DIM = 64
BLOCK = 256
LEVELS = 8
SHARD = 128
ROWS = HEADS * SHARD
LANES = 2 * HEAD_DIM
SCALE = HEAD_DIM**-0.5

SIZES = tuple(max(16, ROWS >> level) for level in range(LEVELS))
STARTS = tuple(sum(SIZES[:level]) for level in range(LEVELS))
TOTAL_ROWS = sum(SIZES)

VMEM = pl.BlockSpec(memory_space=pltpu.VMEM)
SMEM = pl.BlockSpec(memory_space=pltpu.SMEM)
F32 = jnp.float32
BF16 = jnp.bfloat16

NT = (((1,), (1,)), ((), ()))
NN = (((1,), (0,)), ((), ()))
TN = (((0,), (0,)), ((), ()))


def dot(left, right, dims):
    return lax.dot_general(left, right, dims, preferred_element_type=F32)


def shape(rows, kind, *lead):
    return jax.ShapeDtypeStruct(lead + rows, kind)


def low_lanes(rows):
    return lax.broadcasted_iota(jnp.int32, (rows, LANES), 1) < HEAD_DIM


def pool(values, scratch):
    rows = values.shape[0]
    scratch[0:rows, :] = values
    even = scratch[pl.ds(0, rows // 2, stride=2), :]
    odd = scratch[pl.ds(1, rows // 2, stride=2), :]
    return (0.5 * (even + odd)).astype(BF16).astype(F32)


def repeat_rows(values, times, scratch):
    rows = values.shape[0]
    for offset in range(times):
        scratch[pl.ds(offset, rows, stride=times), :] = values
    return scratch[0 : rows * times, :]


def pack_kernel(query_hbm, key_hbm, value_hbm, cot_hbm, out_ref, query_ref, key_ref, value_ref, cot_ref, sems):
    sources = (cot_hbm, query_hbm, value_hbm, key_hbm)
    targets = (cot_ref, query_ref, value_ref, key_ref)
    copies = [pltpu.make_async_copy(source, target, sems.at[n]) for n, (source, target) in enumerate(zip(sources, targets))]
    for copy in copies:
        copy.start()
    for side in range(2):
        copies[2 * side].wait()
        copies[2 * side + 1].wait()
        left, right = targets[2 * side], targets[2 * side + 1]
        for head in range(HEADS):
            columns = slice(head * HEAD_DIM, (head + 1) * HEAD_DIM)
            rows = jnp.concatenate([left[:, columns], right[:, columns]], axis=1)
            out_ref[head, :, LANES * side : LANES * (side + 1)] = rows


def unpack_kernel(in_ref, att_ref, query_ref, key_ref, value_ref):
    for pair in range(HEADS // 2):
        columns = slice(pair * LANES, (pair + 1) * LANES)
        left, right = in_ref[2 * pair], in_ref[2 * pair + 1]
        for place, target in enumerate((att_ref, query_ref, value_ref, key_ref)):
            part = slice(place * HEAD_DIM, (place + 1) * HEAD_DIM)
            target[:, columns] = jnp.concatenate([left[:, part], right[:, part]], axis=1)


def pool_own_kernel(own_ref, level1_ref, level2_ref, level3_ref, scratch):
    level1 = pool(own_ref[:, LANES : 2 * LANES].astype(F32), scratch)
    level1_ref[...] = level1.astype(BF16)
    level2 = pool(level1, scratch)
    level2_ref[...] = level2.astype(BF16)
    level3_ref[...] = pool(level2, scratch).astype(BF16)


def in_order(upper, own, other):
    return jnp.concatenate([jnp.where(upper, other, own), jnp.where(upper, own, other)], axis=0)


def region_kernel(place_ref, own3_ref, sib2_ref, opposite_ref, across_ref, sib3_ref, level4_ref, slots_ref, scratch):
    second, upper = place_ref[0] == 1, place_ref[1] == 1
    own = in_order(second, own3_ref[...].astype(F32), pool(sib2_ref[...].astype(F32), scratch))
    sibling = in_order(second, across_ref[...].astype(F32), opposite_ref[...].astype(F32))
    sib3_ref[...] = sibling.astype(BF16)
    own = pool(own, scratch)
    level4 = in_order(upper, own, pool(sibling, scratch))
    level4_ref[...] = level4.astype(BF16)
    pooled = pool(level4, scratch).astype(BF16)
    for place in range(16):
        slots_ref[place] = pooled


def main_kernel(
    place_ref, own_ref, level1_ref, sib2_ref, sib3_ref, sib4_ref, far_ref,
    front_ref, local_ref, grad2_ref, grad3_ref, grad4_ref, send_ref,
    query_s, sum_s, weight_s, cross_s, upper_s, num_s, high_s, scaled_s, floor_s, sib_s, scr, scr2,
):
    far = place_ref[2]

    def pooled_times(block, times):
        values = block.astype(F32)
        for _ in range(times):
            values = pool(values, scr2)
        return values.astype(BF16)

    for level in range(5, LEVELS):
        count = 2 ** (level - 4)
        base = (far ^ count) & (16 - count)
        part = BLOCK // count
        for child in range(count):
            sib_s[level - 5, part * child : part * (child + 1), :] = pooled_times(far_ref[base + child], level - 5)
    siblings = [sib2_ref, sib3_ref, sib4_ref] + [sib_s.at[number] for number in range(3)]

    values = own_ref[:, 0:LANES].astype(F32)
    for level in range(LEVELS):
        rows = ROWS >> level
        kept = jnp.where(low_lanes(rows), 0.0, values * SCALE)
        if rows < SIZES[level]:
            kept = jnp.concatenate([kept, jnp.zeros((SIZES[level] - rows, LANES), F32)], axis=0)
        query_s[STARTS[level] : STARTS[level] + SIZES[level], :] = kept.astype(BF16)
        if level + 1 < LEVELS:
            values = pool(values, scr)

    tasks = []
    for half in range(2):
        keys = own_ref.at[512 * half : 512 * (half + 1), LANES : 2 * LANES]
        for piece in range(2):
            tasks.append((0, 512 * half + 256 * piece, 256, keys, weight_s.at[2 * half + piece], half))
    for half in range(2):
        keys = level1_ref.at[256 * (1 - half) : 256 * (2 - half), :]
        tasks.append((1, STARTS[1] + 256 * half, 256, keys, cross_s.at[half], half))
    for level in range(2, LEVELS):
        place = STARTS[level] - STARTS[2]
        kept = upper_s.at[place : place + SIZES[level], :]
        tasks.append((level, STARTS[level], SIZES[level], siblings[level - 2], kept, 0))

    for level, first, rows, keys, kept, _ in tasks:
        key_rows = keys[...]
        scores = dot(query_s[first : first + rows, :], key_rows, NT)
        highest = jnp.max(scores, axis=1, keepdims=True)
        weights = jnp.exp(scores - highest).astype(BF16)
        kept[...] = weights
        ones = jnp.ones((key_rows.shape[0], LANES), BF16)
        num_s[first : first + rows, :] = dot(weights, jnp.where(low_lanes(key_rows.shape[0]), key_rows, ones), NN)
        high_s[first : first + rows, :] = jnp.broadcast_to(highest, (rows, LANES))

    rows = ROWS >> (LEVELS - 1)
    peak = high_s[STARTS[-1] : STARTS[-1] + rows, :]
    accum = num_s[STARTS[-1] : STARTS[-1] + rows, :]
    for level in reversed(range(1, LEVELS - 1)):
        peak_up = repeat_rows(peak, 2, scr)
        accum_up = repeat_rows(accum, 2, scr2)
        rows = ROWS >> level
        high = high_s[STARTS[level] : STARTS[level] + rows, :]
        num = num_s[STARTS[level] : STARTS[level] + rows, :]
        peak = jnp.maximum(peak_up, high)
        accum = jnp.exp(peak_up - peak) * accum_up + jnp.exp(high - peak) * num
    repeat_rows(peak, 2, scr)
    repeat_rows(accum, 2, scr2)
    chunk = 128
    low = low_lanes(chunk)
    for first in range(0, ROWS, chunk):
        span = slice(first, first + chunk)
        peak_up, high = scr[span, :], high_s[span, :]
        peak = jnp.maximum(peak_up, high)
        accum = jnp.exp(peak_up - peak) * scr2[span, :] + jnp.exp(high - peak) * num_s[span, :]
        total = jnp.where(low, pltpu.roll(accum, HEAD_DIM, 1), accum)
        attended = (accum / total).astype(BF16)
        front_ref[span, :] = attended
        cot = own_ref[span, 0:LANES].astype(F32)
        drift = jnp.sum(jnp.where(low, cot * attended.astype(F32), 0.0), axis=1, keepdims=True)
        floor_s[span, :] = peak + jnp.log(total)
        scaled_s[span, :] = jnp.where(low, cot, drift)

    for level in range(LEVELS - 1):
        start, rows = STARTS[level], ROWS >> (level + 1)
        even, odd = pl.ds(start, rows, stride=2), pl.ds(start + 1, rows, stride=2)
        floor = jnp.minimum(floor_s[even, :], floor_s[odd, :])
        scaled = jnp.exp(floor - floor_s[even, :]) * scaled_s[even, :] + jnp.exp(floor - floor_s[odd, :]) * scaled_s[odd, :]
        target = slice(STARTS[level + 1], STARTS[level + 1] + rows)
        floor_s[target, :] = floor
        scaled_s[target, :] = scaled
    for level in range(LEVELS):
        start, rows = STARTS[level], ROWS >> level
        for first in range(start, start + rows, 256):
            span = slice(first, first + min(rows, 256))
            scaled = jnp.exp(high_s[span, :] - floor_s[span, :]) * scaled_s[span, :]
            scaled_s[span, :] = scaled
        if rows < SIZES[level]:
            scaled_s[start + rows : start + SIZES[level], :] = jnp.zeros((SIZES[level] - rows, LANES), F32)
    for first in range(0, TOTAL_ROWS, 256):
        span = slice(first, first + 256)
        sum_s[span, :] = jnp.where(low_lanes(256), scaled_s[span, :], 0.0).astype(BF16)

    def gradients(task):
        level, first, rows, keys, kept, _ = task
        span = slice(first, first + rows)
        key_rows = keys[...]
        sums, queries, weights = sum_s[span, :], query_s[span, :], kept[...]
        share_grad = dot(sums, key_rows, NT)
        score_grad = (weights.astype(F32) * (share_grad - scaled_s[span, HEAD_DIM : HEAD_DIM + 1])).astype(BF16)
        query_part = dot(score_grad, key_rows, NN)
        key_part = dot(queries, score_grad, TN) + dot(sums, weights, TN)
        return query_part, key_part

    query_sum = None
    for task in reversed(tasks[6:]):
        query_part, key_part = gradients(task)
        level = task[0]
        rows = ROWS >> level
        query_part = query_part[0:rows, :]
        if query_sum is not None:
            query_part = query_part + 0.5 * repeat_rows(query_sum, 2, scr)
        query_sum = query_part
        key_part = key_part.T
        if level >= 5:
            count = 2 ** (level - 4)
            base = (far ^ count) & (16 - count)
            part = BLOCK // count
            for child in range(count):
                send_ref[base + child, 0:part, :] = key_part[part * child : part * (child + 1), :].astype(BF16)
        elif level == 4:
            grad4_ref[...] = key_part.astype(BF16)
        elif level == 3:
            grad3_ref[...] = key_part.reshape(2, SHARD, LANES)
        else:
            grad2_ref[...] = key_part
    send_ref[far] = jnp.zeros((SHARD, LANES), BF16)
    send_ref[far ^ 1] = jnp.zeros((SHARD, LANES), BF16)

    cross_grads = [gradients(task) for task in tasks[4:6]]
    query_sum = 0.5 * repeat_rows(query_sum, 2, scr) + jnp.concatenate([part[0] for part in cross_grads], axis=0)
    repeat_rows(query_sum, 2, scr)
    repeat_rows(jnp.concatenate([cross_grads[1][1].T, cross_grads[0][1].T], axis=0), 2, scr2)
    for half in range(2):
        total = None
        for task in tasks[2 * half : 2 * half + 2]:
            query_part, key_part = gradients(task)
            span = slice(task[1], task[1] + 256)
            query_part = SCALE * (query_part + 0.5 * scr[span, :])
            front_ref[span, :] = jnp.where(low_lanes(256), front_ref[span, :], query_part.astype(BF16))
            total = key_part if total is None else total + key_part
        span = slice(512 * half, 512 * (half + 1))
        local_ref[span, :] = total.T + 0.5 * scr2[span, :]


def far_grads_kernel(
    place_ref, got_ref, got4_ref, grad2_ref, grad3_ref, own_ref, beside_ref, across_ref, opposite_ref, sums, scr
):
    second, upper, far = place_ref[0], place_ref[1], place_ref[2]
    total = None
    for level in reversed(range(5, LEVELS)):
        count = 2 ** (level - 4)
        base = (far ^ count) & (16 - count)
        part = BLOCK // count
        here = got_ref[base, 0:part, :].astype(F32)
        for child in range(1, count):
            here = here + got_ref[base + child, 0:part, :].astype(F32)
        total = here if total is None else here + 0.5 * repeat_rows(total, 2, scr)
    total = got4_ref[...].astype(F32) + 0.5 * repeat_rows(total, 2, scr)
    sums[...] = total.reshape(4, BLOCK // 4, LANES)
    own = 2 * upper + second
    across_ref[...] = (0.5 * repeat_rows(sums[own ^ 2], 2, scr) + grad3_ref[second]).astype(BF16)
    opposite_ref[...] = 0.5 * repeat_rows(sums[own ^ 3], 2, scr) + grad3_ref[1 - second]
    beside_ref[...] = (0.25 * repeat_rows(sums[own ^ 1], 4, scr) + grad2_ref[...]).astype(BF16)
    own_ref[...] = 0.25 * repeat_rows(sums[own], 4, scr)


def relay_kernel(own_ref, got_ref, out_ref):
    out_ref[...] = (own_ref[...] + got_ref[...].astype(F32)).astype(BF16)


def own_grads_kernel(beside_ref, opposite_ref, kept_ref, local_ref, front_ref, out_ref, scr):
    total = kept_ref[...] + beside_ref[...].astype(F32)
    total = total + 0.5 * repeat_rows(opposite_ref[...].astype(F32), 2, scr)
    repeat_rows(total, 4, scr)
    for head in range(HEADS):
        span = slice(head * SHARD, (head + 1) * SHARD)
        out_ref[head, :, 0:LANES] = front_ref[span, :]
        out_ref[head, :, LANES : 2 * LANES] = (local_ref[span, :] + 0.25 * scr[span, :]).astype(BF16)


def call(kernel, outs, scratch, megabytes, in_specs):
    return pl.pallas_call(
        kernel,
        out_shape=outs,
        in_specs=in_specs,
        out_specs=jax.tree.map(lambda _: VMEM, outs),
        scratch_shapes=scratch,
        compiler_params=pltpu.CompilerParams(vmem_limit_bytes=megabytes * 2**20),
    )


def wide(rows):
    return pltpu.VMEM((rows, LANES), F32)


def on_device(far_groups, head_groups, queries, key_tokens, value_tokens, cotangent):
    seq_place, grp_place = lax.axis_index("seq"), lax.axis_index("grp")
    far_place = (seq_place >> 5 & 3) | grp_place << 2
    place = jnp.stack([seq_place >> 3 & 1, seq_place >> 4 & 1, far_place]).astype(jnp.int32)
    block, block32 = shape((BLOCK, LANES), BF16), shape((BLOCK, LANES), F32)
    packed_shape = shape((HEADS, SHARD, 2 * LANES), BF16)

    def exchange(slots, groups):
        return lax.all_to_all(slots, ("grp", "seq"), 0, 0, axis_index_groups=groups)

    def swap(rows, mask):
        return lax.ppermute(rows, "seq", [(source, source ^ mask) for source in range(lax.axis_size("seq"))])

    packed = call(
        pack_kernel,
        packed_shape,
        [pltpu.VMEM((SHARD, HEADS * HEAD_DIM), BF16)] * 4 + [pltpu.SemaphoreType.DMA((4,))],
        60,
        [pl.BlockSpec(memory_space=pl.ANY)] * 4,
    )(queries, key_tokens, value_tokens, cotangent)
    own = exchange(packed, head_groups).reshape(ROWS, 2 * LANES)
    half = shape((SHARD, LANES), BF16)
    level1, level2, level3 = call(
        pool_own_kernel, (shape((512, LANES), BF16), block, half), [wide(ROWS)], 8, [VMEM]
    )(own)
    opposite = swap(level3, 24)
    sib2 = swap(level2, 8)
    across = swap(opposite, 8)
    sib3, level4, slots = call(
        region_kernel, (block, block, shape((16, SHARD, LANES), BF16)), [wide(BLOCK)], 8, [SMEM] + [VMEM] * 4
    )(place, level3, sib2, opposite, across)
    sib4 = swap(level4, 32)
    far_rows = exchange(slots, far_groups)
    upper_rows = TOTAL_ROWS - STARTS[2]
    front, local, grad2, grad3, grad4, slots = call(
        main_kernel,
        (
            shape((ROWS, LANES), BF16),
            shape((ROWS, LANES), F32),
            block32,
            shape((2, SHARD, LANES), F32),
            block,
            shape((16, SHARD, LANES), BF16),
        ),
        [
            pltpu.VMEM((TOTAL_ROWS, LANES), BF16),
            pltpu.VMEM((TOTAL_ROWS, LANES), BF16),
            pltpu.VMEM((4, 256, 512), BF16),
            pltpu.VMEM((2, 256, 256), BF16),
            pltpu.VMEM((upper_rows, 256), BF16),
            wide(TOTAL_ROWS),
            wide(TOTAL_ROWS),
            wide(TOTAL_ROWS),
            wide(TOTAL_ROWS),
            pltpu.VMEM((3, BLOCK, LANES), BF16),
            wide(ROWS),
            wide(ROWS),
        ],
        32,
        [SMEM] + [VMEM] * 6,
    )(place, own, level1, sib2, sib3, sib4, far_rows)
    got4 = swap(grad4, 32)
    kept, beside, across, opposite = call(
        far_grads_kernel,
        (block32, block, half, shape((SHARD, LANES), F32)),
        [pltpu.VMEM((4, BLOCK // 4, LANES), F32), wide(BLOCK)],
        8,
        [SMEM] + [VMEM] * 4,
    )(place, exchange(slots, far_groups), got4, grad2, grad3)
    relayed = call(relay_kernel, half, [], 8, [VMEM] * 2)(opposite, swap(across, 8))
    packed = call(own_grads_kernel, packed_shape, [wide(ROWS)], 8, [VMEM] * 5)(
        swap(beside, 8), swap(relayed, 24), kept, local, front
    )
    return call(unpack_kernel, (shape((SHARD, HEADS * HEAD_DIM), BF16),) * 4, [], 8, [VMEM])(
        exchange(packed, head_groups)
    )


def groups_over(bits, devices):
    mask = sum(1 << bit for bit in bits)
    offsets = [sum((number >> order & 1) << bit for order, bit in enumerate(bits)) for number in range(2 ** len(bits))]
    return [[base + offset for offset in offsets] for base in range(devices) if base & mask == 0]


def solution(mesh):
    devices = mesh.size
    spec = P(("grp", "seq"), None)
    return jax.shard_map(
        functools.partial(
            on_device,
            groups_over((5, 6, 7, 8), devices),
            groups_over((0, 1, 2), devices),
        ),
        mesh=mesh,
        in_specs=(spec,) * 4,
        out_specs=(spec,) * 4,
        check_vma=False,
    )
```

```python
import functools

import jax
import jax.numpy as jnp
from jax import lax
from jax.experimental import pallas as pl
from jax.experimental.pallas import tpu as pltpu
from jax.sharding import PartitionSpec as P

HEADS = 8
HEAD_DIM = 64
BLOCK = 256
LEVELS = 8
SHARD = 128
ROWS = HEADS * SHARD
LANES = 2 * HEAD_DIM
SCALE = HEAD_DIM**-0.5

SIZES = tuple(max(16, ROWS >> level) for level in range(LEVELS))
STARTS = tuple(sum(SIZES[:level]) for level in range(LEVELS))
TOTAL_ROWS = sum(SIZES)

VMEM = pl.BlockSpec(memory_space=pltpu.VMEM)
SMEM = pl.BlockSpec(memory_space=pltpu.SMEM)
F32 = jnp.float32
BF16 = jnp.bfloat16

NT = (((1,), (1,)), ((), ()))
NN = (((1,), (0,)), ((), ()))
TN = (((0,), (0,)), ((), ()))


def dot(left, right, dims):
    return lax.dot_general(left, right, dims, preferred_element_type=F32)


def shape(rows, kind, *lead):
    return jax.ShapeDtypeStruct(lead + rows, kind)


def low_lanes(rows):
    return lax.broadcasted_iota(jnp.int32, (rows, LANES), 1) < HEAD_DIM


def pool(values, scratch):
    rows = values.shape[0]
    scratch[0:rows, :] = values
    even = scratch[pl.ds(0, rows // 2, stride=2), :]
    odd = scratch[pl.ds(1, rows // 2, stride=2), :]
    return (0.5 * (even + odd)).astype(BF16).astype(F32)


def repeat_rows(values, times, scratch):
    rows = values.shape[0]
    for offset in range(times):
        scratch[pl.ds(offset, rows, stride=times), :] = values
    return scratch[0 : rows * times, :]


def pack_kernel(query_hbm, key_hbm, value_hbm, cot_hbm, out_ref, query_ref, key_ref, value_ref, cot_ref, sems):
    sources = (cot_hbm, query_hbm, value_hbm, key_hbm)
    targets = (cot_ref, query_ref, value_ref, key_ref)
    copies = [pltpu.make_async_copy(source, target, sems.at[n]) for n, (source, target) in enumerate(zip(sources, targets))]
    for copy in copies:
        copy.start()
    for side in range(2):
        copies[2 * side].wait()
        copies[2 * side + 1].wait()
        left, right = targets[2 * side], targets[2 * side + 1]
        for head in range(HEADS):
            columns = slice(head * HEAD_DIM, (head + 1) * HEAD_DIM)
            rows = jnp.concatenate([left[:, columns], right[:, columns]], axis=1)
            out_ref[head, :, LANES * side : LANES * (side + 1)] = rows


def unpack_kernel(in_ref, att_ref, query_ref, key_ref, value_ref):
    for pair in range(HEADS // 2):
        columns = slice(pair * LANES, (pair + 1) * LANES)
        left, right = in_ref[2 * pair], in_ref[2 * pair + 1]
        for place, target in enumerate((att_ref, query_ref, value_ref, key_ref)):
            part = slice(place * HEAD_DIM, (place + 1) * HEAD_DIM)
            target[:, columns] = jnp.concatenate([left[:, part], right[:, part]], axis=1)


def pool_own_kernel(own_ref, level1_ref, level2_ref, level3_ref, scratch):
    level1 = pool(own_ref[:, LANES : 2 * LANES].astype(F32), scratch)
    level1_ref[...] = level1.astype(BF16)
    level2 = pool(level1, scratch)
    level2_ref[...] = level2.astype(BF16)
    level3_ref[...] = pool(level2, scratch).astype(BF16)


def in_order(upper, own, other):
    return jnp.concatenate([jnp.where(upper, other, own), jnp.where(upper, own, other)], axis=0)


def region_kernel(place_ref, own3_ref, sib2_ref, opposite_ref, across_ref, sib3_ref, level4_ref, slots_ref, scratch):
    second, upper = place_ref[0] == 1, place_ref[1] == 1
    own = in_order(second, own3_ref[...].astype(F32), pool(sib2_ref[...].astype(F32), scratch))
    sibling = in_order(second, across_ref[...].astype(F32), opposite_ref[...].astype(F32))
    sib3_ref[...] = sibling.astype(BF16)
    own = pool(own, scratch)
    level4 = in_order(upper, own, pool(sibling, scratch))
    level4_ref[...] = level4.astype(BF16)
    pooled = pool(level4, scratch).astype(BF16)
    for place in range(16):
        slots_ref[place] = pooled


def main_kernel(
    place_ref, own_ref, level1_ref, sib2_ref, sib3_ref, sib4_ref, far_ref,
    front_ref, local_ref, grad2_ref, grad3_ref, grad4_ref, send_ref,
    query_s, sum_s, weight_s, cross_s, upper_s, num_s, high_s, scaled_s, floor_s, sib_s, scr, scr2,
):
    far = place_ref[2]

    def pooled_times(block, times):
        values = block.astype(F32)
        for _ in range(times):
            values = pool(values, scr2)
        return values.astype(BF16)

    for level in range(5, LEVELS):
        count = 2 ** (level - 4)
        base = (far ^ count) & (16 - count)
        part = BLOCK // count
        for child in range(count):
            sib_s[level - 5, part * child : part * (child + 1), :] = pooled_times(far_ref[base + child], level - 5)
    siblings = [sib2_ref, sib3_ref, sib4_ref] + [sib_s.at[number] for number in range(3)]

    values = own_ref[:, 0:LANES].astype(F32)
    for level in range(LEVELS):
        rows = ROWS >> level
        kept = jnp.where(low_lanes(rows), 0.0, values * SCALE)
        if rows < SIZES[level]:
            kept = jnp.concatenate([kept, jnp.zeros((SIZES[level] - rows, LANES), F32)], axis=0)
        query_s[STARTS[level] : STARTS[level] + SIZES[level], :] = kept.astype(BF16)
        if level + 1 < LEVELS:
            values = pool(values, scr)

    tasks = []
    for half in range(2):
        keys = own_ref.at[512 * half : 512 * (half + 1), LANES : 2 * LANES]
        for piece in range(2):
            tasks.append((0, 512 * half + 256 * piece, 256, keys, weight_s.at[2 * half + piece], half))
    for half in range(2):
        keys = level1_ref.at[256 * (1 - half) : 256 * (2 - half), :]
        tasks.append((1, STARTS[1] + 256 * half, 256, keys, cross_s.at[half], half))
    for level in range(2, LEVELS):
        place = STARTS[level] - STARTS[2]
        kept = upper_s.at[place : place + SIZES[level], :]
        tasks.append((level, STARTS[level], SIZES[level], siblings[level - 2], kept, 0))

    for level, first, rows, keys, kept, _ in tasks:
        key_rows = keys[...]
        scores = dot(query_s[first : first + rows, :], key_rows, NT)
        highest = jnp.max(scores, axis=1, keepdims=True)
        weights = jnp.exp(scores - highest).astype(BF16)
        kept[...] = weights
        ones = jnp.ones((key_rows.shape[0], LANES), BF16)
        num_s[first : first + rows, :] = dot(weights, jnp.where(low_lanes(key_rows.shape[0]), key_rows, ones), NN)
        high_s[first : first + rows, :] = jnp.broadcast_to(highest, (rows, LANES))

    rows = ROWS >> (LEVELS - 1)
    peak = high_s[STARTS[-1] : STARTS[-1] + rows, :]
    accum = num_s[STARTS[-1] : STARTS[-1] + rows, :]
    for level in reversed(range(1, LEVELS - 1)):
        peak_up = repeat_rows(peak, 2, scr)
        accum_up = repeat_rows(accum, 2, scr2)
        rows = ROWS >> level
        high = high_s[STARTS[level] : STARTS[level] + rows, :]
        num = num_s[STARTS[level] : STARTS[level] + rows, :]
        peak = jnp.maximum(peak_up, high)
        accum = jnp.exp(peak_up - peak) * accum_up + jnp.exp(high - peak) * num
    repeat_rows(peak, 2, scr)
    repeat_rows(accum, 2, scr2)
    chunk = 128
    low = low_lanes(chunk)
    for first in range(0, ROWS, chunk):
        span = slice(first, first + chunk)
        peak_up, high = scr[span, :], high_s[span, :]
        peak = jnp.maximum(peak_up, high)
        accum = jnp.exp(peak_up - peak) * scr2[span, :] + jnp.exp(high - peak) * num_s[span, :]
        total = jnp.where(low, pltpu.roll(accum, HEAD_DIM, 1), accum)
        attended = (accum / total).astype(BF16)
        front_ref[span, :] = attended
        cot = own_ref[span, 0:LANES].astype(F32)
        drift = jnp.sum(jnp.where(low, cot * attended.astype(F32), 0.0), axis=1, keepdims=True)
        floor_s[span, :] = peak + jnp.log(total)
        scaled_s[span, :] = jnp.where(low, cot, drift)

    for level in range(LEVELS - 1):
        start, rows = STARTS[level], ROWS >> (level + 1)
        even, odd = pl.ds(start, rows, stride=2), pl.ds(start + 1, rows, stride=2)
        floor = jnp.minimum(floor_s[even, :], floor_s[odd, :])
        scaled = jnp.exp(floor - floor_s[even, :]) * scaled_s[even, :] + jnp.exp(floor - floor_s[odd, :]) * scaled_s[odd, :]
        target = slice(STARTS[level + 1], STARTS[level + 1] + rows)
        floor_s[target, :] = floor
        scaled_s[target, :] = scaled
    for level in range(LEVELS):
        start, rows = STARTS[level], ROWS >> level
        for first in range(start, start + rows, 256):
            span = slice(first, first + min(rows, 256))
            scaled = jnp.exp(high_s[span, :] - floor_s[span, :]) * scaled_s[span, :]
            scaled_s[span, :] = scaled
        if rows < SIZES[level]:
            scaled_s[start + rows : start + SIZES[level], :] = jnp.zeros((SIZES[level] - rows, LANES), F32)
    for first in range(0, TOTAL_ROWS, 256):
        span = slice(first, first + 256)
        sum_s[span, :] = jnp.where(low_lanes(256), scaled_s[span, :], 0.0).astype(BF16)

    def gradients(task):
        level, first, rows, keys, kept, _ = task
        span = slice(first, first + rows)
        key_rows = keys[...]
        sums, queries, weights = sum_s[span, :], query_s[span, :], kept[...]
        share_grad = dot(sums, key_rows, NT)
        score_grad = (weights.astype(F32) * (share_grad - scaled_s[span, HEAD_DIM : HEAD_DIM + 1])).astype(BF16)
        query_part = dot(score_grad, key_rows, NN)
        key_part = dot(queries, score_grad, TN) + dot(sums, weights, TN)
        return query_part, key_part

    query_sum = None
    for task in reversed(tasks[6:]):
        query_part, key_part = gradients(task)
        level = task[0]
        rows = ROWS >> level
        query_part = query_part[0:rows, :]
        if query_sum is not None:
            query_part = query_part + 0.5 * repeat_rows(query_sum, 2, scr)
        query_sum = query_part
        key_part = key_part.T
        if level >= 5:
            count = 2 ** (level - 4)
            base = (far ^ count) & (16 - count)
            part = BLOCK // count
            for child in range(count):
                send_ref[base + child, 0:part, :] = key_part[part * child : part * (child + 1), :].astype(BF16)
        elif level == 4:
            grad4_ref[...] = key_part.astype(BF16)
        elif level == 3:
            grad3_ref[...] = key_part.reshape(2, SHARD, LANES)
        else:
            grad2_ref[...] = key_part
    send_ref[far] = jnp.zeros((SHARD, LANES), BF16)
    send_ref[far ^ 1] = jnp.zeros((SHARD, LANES), BF16)

    cross_grads = [gradients(task) for task in tasks[4:6]]
    query_sum = 0.5 * repeat_rows(query_sum, 2, scr) + jnp.concatenate([part[0] for part in cross_grads], axis=0)
    repeat_rows(query_sum, 2, scr)
    repeat_rows(jnp.concatenate([cross_grads[1][1].T, cross_grads[0][1].T], axis=0), 2, scr2)
    for half in range(2):
        total = None
        for task in tasks[2 * half : 2 * half + 2]:
            query_part, key_part = gradients(task)
            span = slice(task[1], task[1] + 256)
            query_part = SCALE * (query_part + 0.5 * scr[span, :])
            front_ref[span, :] = jnp.where(low_lanes(256), front_ref[span, :], query_part.astype(BF16))
            total = key_part if total is None else total + key_part
        span = slice(512 * half, 512 * (half + 1))
        local_ref[span, :] = total.T + 0.5 * scr2[span, :]


def far_grads_kernel(
    place_ref, got_ref, got4_ref, grad2_ref, grad3_ref, own_ref, beside_ref, across_ref, opposite_ref, sums, scr
):
    second, upper, far = place_ref[0], place_ref[1], place_ref[2]
    total = None
    for level in reversed(range(5, LEVELS)):
        count = 2 ** (level - 4)
        base = (far ^ count) & (16 - count)
        part = BLOCK // count
        here = got_ref[base, 0:part, :].astype(F32)
        for child in range(1, count):
            here = here + got_ref[base + child, 0:part, :].astype(F32)
        total = here if total is None else here + 0.5 * repeat_rows(total, 2, scr)
    total = got4_ref[...].astype(F32) + 0.5 * repeat_rows(total, 2, scr)
    sums[...] = total.reshape(4, BLOCK // 4, LANES)
    own = 2 * upper + second
    across_ref[...] = (0.5 * repeat_rows(sums[own ^ 2], 2, scr) + grad3_ref[second]).astype(BF16)
    opposite_ref[...] = 0.5 * repeat_rows(sums[own ^ 3], 2, scr) + grad3_ref[1 - second]
    beside_ref[...] = (0.25 * repeat_rows(sums[own ^ 1], 4, scr) + grad2_ref[...]).astype(BF16)
    own_ref[...] = 0.25 * repeat_rows(sums[own], 4, scr)


def relay_kernel(own_ref, got_ref, out_ref):
    out_ref[...] = (own_ref[...] + got_ref[...].astype(F32)).astype(BF16)


def own_grads_kernel(beside_ref, opposite_ref, kept_ref, local_ref, front_ref, out_ref, scr):
    total = kept_ref[...] + beside_ref[...].astype(F32)
    total = total + 0.5 * repeat_rows(opposite_ref[...].astype(F32), 2, scr)
    repeat_rows(total, 4, scr)
    for head in range(HEADS):
        span = slice(head * SHARD, (head + 1) * SHARD)
        out_ref[head, :, 0:LANES] = front_ref[span, :]
        out_ref[head, :, LANES : 2 * LANES] = (local_ref[span, :] + 0.25 * scr[span, :]).astype(BF16)


def call(kernel, outs, scratch, megabytes, in_specs):
    return pl.pallas_call(
        kernel,
        out_shape=outs,
        in_specs=in_specs,
        out_specs=jax.tree.map(lambda _: VMEM, outs),
        scratch_shapes=scratch,
        compiler_params=pltpu.CompilerParams(vmem_limit_bytes=megabytes * 2**20),
    )


def wide(rows):
    return pltpu.VMEM((rows + 8, LANES), F32)


def on_device(far_groups, head_groups, queries, key_tokens, value_tokens, cotangent):
    seq_place, grp_place = lax.axis_index("seq"), lax.axis_index("grp")
    far_place = (seq_place >> 5 & 3) | grp_place << 2
    place = jnp.stack([seq_place >> 3 & 1, seq_place >> 4 & 1, far_place]).astype(jnp.int32)
    block, block32 = shape((BLOCK, LANES), BF16), shape((BLOCK, LANES), F32)
    packed_shape = shape((HEADS, SHARD, 2 * LANES), BF16)

    def exchange(slots, groups):
        return lax.all_to_all(slots, ("grp", "seq"), 0, 0, axis_index_groups=groups)

    def swap(rows, mask):
        return lax.ppermute(rows, "seq", [(source, source ^ mask) for source in range(lax.axis_size("seq"))])

    packed = call(
        pack_kernel,
        packed_shape,
        [pltpu.VMEM((SHARD, HEADS * HEAD_DIM), BF16)] * 4 + [pltpu.SemaphoreType.DMA((4,))],
        60,
        [pl.BlockSpec(memory_space=pl.ANY)] * 4,
    )(queries, key_tokens, value_tokens, cotangent)
    own = exchange(packed, head_groups).reshape(ROWS, 2 * LANES)
    half = shape((SHARD, LANES), BF16)
    level1, level2, level3 = call(
        pool_own_kernel, (shape((512, LANES), BF16), block, half), [wide(ROWS)], 8, [VMEM]
    )(own)
    opposite = swap(level3, 24)
    sib2 = swap(level2, 8)
    across = swap(opposite, 8)
    sib3, level4, slots = call(
        region_kernel, (block, block, shape((16, SHARD, LANES), BF16)), [wide(BLOCK)], 8, [SMEM] + [VMEM] * 4
    )(place, level3, sib2, opposite, across)
    sib4 = swap(level4, 32)
    far_rows = exchange(slots, far_groups)
    upper_rows = TOTAL_ROWS - STARTS[2]
    front, local, grad2, grad3, grad4, slots = call(
        main_kernel,
        (
            shape((ROWS, LANES), BF16),
            shape((ROWS, LANES), F32),
            block32,
            shape((2, SHARD, LANES), F32),
            block,
            shape((16, SHARD, LANES), BF16),
        ),
        [
            pltpu.VMEM((TOTAL_ROWS, LANES), BF16),
            pltpu.VMEM((TOTAL_ROWS, LANES), BF16),
            pltpu.VMEM((4, 256, 512), BF16),
            pltpu.VMEM((2, 256, 256), BF16),
            pltpu.VMEM((upper_rows, 256), BF16),
            wide(TOTAL_ROWS),
            wide(TOTAL_ROWS),
            wide(TOTAL_ROWS),
            wide(TOTAL_ROWS),
            pltpu.VMEM((3, BLOCK, LANES), BF16),
            wide(ROWS),
            wide(ROWS),
        ],
        32,
        [SMEM] + [VMEM] * 6,
    )(place, own, level1, sib2, sib3, sib4, far_rows)
    got4 = swap(grad4, 32)
    kept, beside, across, opposite = call(
        far_grads_kernel,
        (block32, block, half, shape((SHARD, LANES), F32)),
        [pltpu.VMEM((4, BLOCK // 4, LANES), F32), wide(BLOCK)],
        8,
        [SMEM] + [VMEM] * 4,
    )(place, exchange(slots, far_groups), got4, grad2, grad3)
    relayed = call(relay_kernel, half, [], 8, [VMEM] * 2)(opposite, swap(across, 8))
    packed = call(own_grads_kernel, packed_shape, [wide(ROWS)], 8, [VMEM] * 5)(
        swap(beside, 8), swap(relayed, 24), kept, local, front
    )
    return call(unpack_kernel, (shape((SHARD, HEADS * HEAD_DIM), BF16),) * 4, [], 8, [VMEM])(
        exchange(packed, head_groups)
    )


def groups_over(bits, devices):
    mask = sum(1 << bit for bit in bits)
    offsets = [sum((number >> order & 1) << bit for order, bit in enumerate(bits)) for number in range(2 ** len(bits))]
    return [[base + offset for offset in offsets] for base in range(devices) if base & mask == 0]


def solution(mesh):
    devices = mesh.size
    spec = P(("grp", "seq"), None)
    return jax.shard_map(
        functools.partial(
            on_device,
            groups_over((5, 6, 7, 8), devices),
            groups_over((0, 1, 2), devices),
        ),
        mesh=mesh,
        in_specs=(spec,) * 4,
        out_specs=(spec,) * 4,
        check_vma=False,
    )
```

```python
import functools

import jax
import jax.numpy as jnp
from jax import lax
from jax.experimental import pallas as pl
from jax.experimental.pallas import tpu as pltpu
from jax.sharding import PartitionSpec as P

HEADS = 8
HEAD_DIM = 64
BLOCK = 256
LEVELS = 8
SHARD = 128
ROWS = HEADS * SHARD
LANES = 2 * HEAD_DIM
SCALE = HEAD_DIM**-0.5

SIZES = tuple(max(16, ROWS >> level) for level in range(LEVELS))
STARTS = tuple(sum(SIZES[:level]) for level in range(LEVELS))
TOTAL_ROWS = sum(SIZES)

VMEM = pl.BlockSpec(memory_space=pltpu.VMEM)
SMEM = pl.BlockSpec(memory_space=pltpu.SMEM)
F32 = jnp.float32
BF16 = jnp.bfloat16

NT = (((1,), (1,)), ((), ()))
NN = (((1,), (0,)), ((), ()))
TN = (((0,), (0,)), ((), ()))


def dot(left, right, dims):
    return lax.dot_general(left, right, dims, preferred_element_type=F32)


def shape(rows, kind, *lead):
    return jax.ShapeDtypeStruct(lead + rows, kind)


def low_lanes(rows):
    return lax.broadcasted_iota(jnp.int32, (rows, LANES), 1) < HEAD_DIM


def pool(values, scratch):
    rows = values.shape[0]
    scratch[0:rows, :] = values
    even = scratch[pl.ds(0, rows // 2, stride=2), :]
    odd = scratch[pl.ds(1, rows // 2, stride=2), :]
    return (0.5 * (even + odd)).astype(BF16).astype(F32)


def repeat_rows(values, times, scratch):
    rows = values.shape[0]
    for offset in range(times):
        scratch[pl.ds(offset, rows, stride=times), :] = values
    return scratch[0 : rows * times, :]


def pack_kernel(query_hbm, key_hbm, value_hbm, cot_hbm, out_ref, query_ref, key_ref, value_ref, cot_ref, sems):
    sources = (cot_hbm, query_hbm, value_hbm, key_hbm)
    targets = (cot_ref, query_ref, value_ref, key_ref)
    copies = [pltpu.make_async_copy(source, target, sems.at[n]) for n, (source, target) in enumerate(zip(sources, targets))]
    for copy in copies:
        copy.start()
    for side in range(2):
        copies[2 * side].wait()
        copies[2 * side + 1].wait()
        left, right = targets[2 * side], targets[2 * side + 1]
        for head in range(HEADS):
            columns = slice(head * HEAD_DIM, (head + 1) * HEAD_DIM)
            rows = jnp.concatenate([left[:, columns], right[:, columns]], axis=1)
            out_ref[head, :, LANES * side : LANES * (side + 1)] = rows


def unpack_kernel(in_ref, att_hbm, query_hbm, key_hbm, value_hbm, att_ref, query_ref, key_ref, value_ref, sems):
    targets = ((att_ref, att_hbm), (query_ref, query_hbm), (value_ref, value_hbm), (key_ref, key_hbm))
    copies = []
    for place, (target, output) in enumerate(targets):
        part = slice(place * HEAD_DIM, (place + 1) * HEAD_DIM)
        for pair in range(HEADS // 2):
            columns = slice(pair * LANES, (pair + 1) * LANES)
            target[:, columns] = jnp.concatenate([in_ref[2 * pair, :, part], in_ref[2 * pair + 1, :, part]], axis=1)
        copies.append(pltpu.make_async_copy(target, output, sems.at[place]))
        copies[-1].start()
    for copy in copies:
        copy.wait()


def pool_own_kernel(own_ref, level1_ref, level2_ref, level3_ref, scratch):
    level1 = pool(own_ref[:, LANES : 2 * LANES].astype(F32), scratch)
    level1_ref[...] = level1.astype(BF16)
    level2 = pool(level1, scratch)
    level2_ref[...] = level2.astype(BF16)
    level3_ref[...] = pool(level2, scratch).astype(BF16)


def in_order(upper, own, other):
    return jnp.concatenate([jnp.where(upper, other, own), jnp.where(upper, own, other)], axis=0)


def region_kernel(place_ref, own3_ref, sib2_ref, opposite_ref, across_ref, sib3_ref, level4_ref, slots_ref, scratch):
    second, upper = place_ref[0] == 1, place_ref[1] == 1
    own = in_order(second, own3_ref[...].astype(F32), pool(sib2_ref[...].astype(F32), scratch))
    sibling = in_order(second, across_ref[...].astype(F32), opposite_ref[...].astype(F32))
    sib3_ref[...] = sibling.astype(BF16)
    own = pool(own, scratch)
    level4 = in_order(upper, own, pool(sibling, scratch))
    level4_ref[...] = level4.astype(BF16)
    pooled = pool(level4, scratch).astype(BF16)
    for place in range(16):
        slots_ref[place] = pooled


def main_kernel(
    place_ref, own_ref, level1_ref, sib2_ref, sib3_ref, sib4_ref, far_ref,
    front_ref, local_ref, grad2_ref, grad3_ref, grad4_ref, send_ref,
    query_s, sum_s, weight_s, cross_s, upper_s, num_s, high_s, scaled_s, floor_s, sib_s, scr, scr2,
):
    far = place_ref[2]

    def pooled_times(block, times):
        values = block.astype(F32)
        for _ in range(times):
            values = pool(values, scr2)
        return values.astype(BF16)

    for level in range(5, LEVELS):
        count = 2 ** (level - 4)
        base = (far ^ count) & (16 - count)
        part = BLOCK // count
        for child in range(count):
            sib_s[level - 5, part * child : part * (child + 1), :] = pooled_times(far_ref[base + child], level - 5)
    siblings = [sib2_ref, sib3_ref, sib4_ref] + [sib_s.at[number] for number in range(3)]

    values = own_ref[:, 0:LANES].astype(F32)
    for level in range(LEVELS):
        rows = ROWS >> level
        kept = jnp.where(low_lanes(rows), 0.0, values * SCALE)
        if rows < SIZES[level]:
            kept = jnp.concatenate([kept, jnp.zeros((SIZES[level] - rows, LANES), F32)], axis=0)
        query_s[STARTS[level] : STARTS[level] + SIZES[level], :] = kept.astype(BF16)
        if level + 1 < LEVELS:
            values = pool(values, scr)

    tasks = []
    for half in range(2):
        keys = own_ref.at[512 * half : 512 * (half + 1), LANES : 2 * LANES]
        for piece in range(2):
            tasks.append((0, 512 * half + 256 * piece, 256, keys, weight_s.at[2 * half + piece], half))
    for half in range(2):
        keys = level1_ref.at[256 * (1 - half) : 256 * (2 - half), :]
        tasks.append((1, STARTS[1] + 256 * half, 256, keys, cross_s.at[half], half))
    for level in range(2, LEVELS):
        place = STARTS[level] - STARTS[2]
        kept = upper_s.at[place : place + SIZES[level], :]
        tasks.append((level, STARTS[level], SIZES[level], siblings[level - 2], kept, 0))

    for level, first, rows, keys, kept, _ in tasks:
        key_rows = keys[...]
        scores = dot(query_s[first : first + rows, :], key_rows, NT)
        highest = jnp.max(scores, axis=1, keepdims=True)
        weights = jnp.exp(scores - highest).astype(BF16)
        kept[...] = weights
        ones = jnp.ones((key_rows.shape[0], LANES), BF16)
        num_s[first : first + rows, :] = dot(weights, jnp.where(low_lanes(key_rows.shape[0]), key_rows, ones), NN)
        high_s[first : first + rows, :] = jnp.broadcast_to(highest, (rows, LANES))

    rows = ROWS >> (LEVELS - 1)
    peak = high_s[STARTS[-1] : STARTS[-1] + rows, :]
    accum = num_s[STARTS[-1] : STARTS[-1] + rows, :]
    for level in reversed(range(1, LEVELS - 1)):
        peak_up = repeat_rows(peak, 2, scr)
        accum_up = repeat_rows(accum, 2, scr2)
        rows = ROWS >> level
        high = high_s[STARTS[level] : STARTS[level] + rows, :]
        num = num_s[STARTS[level] : STARTS[level] + rows, :]
        peak = jnp.maximum(peak_up, high)
        accum = jnp.exp(peak_up - peak) * accum_up + jnp.exp(high - peak) * num
    repeat_rows(peak, 2, scr)
    repeat_rows(accum, 2, scr2)
    chunk = 128
    low = low_lanes(chunk)
    for first in range(0, ROWS, chunk):
        span = slice(first, first + chunk)
        peak_up, high = scr[span, :], high_s[span, :]
        peak = jnp.maximum(peak_up, high)
        accum = jnp.exp(peak_up - peak) * scr2[span, :] + jnp.exp(high - peak) * num_s[span, :]
        total = jnp.where(low, pltpu.roll(accum, HEAD_DIM, 1), accum)
        attended = (accum / total).astype(BF16)
        front_ref[span, :] = attended
        cot = own_ref[span, 0:LANES].astype(F32)
        drift = jnp.sum(jnp.where(low, cot * attended.astype(F32), 0.0), axis=1, keepdims=True)
        floor_s[span, :] = peak + jnp.log(total)
        scaled_s[span, :] = jnp.where(low, cot, drift)

    for level in range(LEVELS - 1):
        start, rows = STARTS[level], ROWS >> (level + 1)
        even, odd = pl.ds(start, rows, stride=2), pl.ds(start + 1, rows, stride=2)
        floor = jnp.minimum(floor_s[even, :], floor_s[odd, :])
        scaled = jnp.exp(floor - floor_s[even, :]) * scaled_s[even, :] + jnp.exp(floor - floor_s[odd, :]) * scaled_s[odd, :]
        target = slice(STARTS[level + 1], STARTS[level + 1] + rows)
        floor_s[target, :] = floor
        scaled_s[target, :] = scaled
    for level in range(LEVELS):
        start, rows = STARTS[level], ROWS >> level
        for first in range(start, start + rows, 256):
            span = slice(first, first + min(rows, 256))
            scaled = jnp.exp(high_s[span, :] - floor_s[span, :]) * scaled_s[span, :]
            scaled_s[span, :] = scaled
        if rows < SIZES[level]:
            scaled_s[start + rows : start + SIZES[level], :] = jnp.zeros((SIZES[level] - rows, LANES), F32)
    for first in range(0, TOTAL_ROWS, 256):
        span = slice(first, first + 256)
        sum_s[span, :] = jnp.where(low_lanes(256), scaled_s[span, :], 0.0).astype(BF16)

    def gradients(task):
        level, first, rows, keys, kept, _ = task
        span = slice(first, first + rows)
        key_rows = keys[...]
        sums, queries, weights = sum_s[span, :], query_s[span, :], kept[...]
        share_grad = dot(sums, key_rows, NT)
        score_grad = (weights.astype(F32) * (share_grad - scaled_s[span, HEAD_DIM : HEAD_DIM + 1])).astype(BF16)
        query_part = dot(score_grad, key_rows, NN)
        key_part = dot(queries, score_grad, TN) + dot(sums, weights, TN)
        return query_part, key_part

    query_sum = None
    for task in reversed(tasks[6:]):
        query_part, key_part = gradients(task)
        level = task[0]
        rows = ROWS >> level
        query_part = query_part[0:rows, :]
        if query_sum is not None:
            query_part = query_part + 0.5 * repeat_rows(query_sum, 2, scr)
        query_sum = query_part
        key_part = key_part.T
        if level >= 5:
            count = 2 ** (level - 4)
            base = (far ^ count) & (16 - count)
            part = BLOCK // count
            for child in range(count):
                send_ref[base + child, 0:part, :] = key_part[part * child : part * (child + 1), :].astype(BF16)
        elif level == 4:
            grad4_ref[...] = key_part.astype(BF16)
        elif level == 3:
            grad3_ref[...] = key_part.reshape(2, SHARD, LANES)
        else:
            grad2_ref[...] = key_part
    send_ref[far] = jnp.zeros((SHARD, LANES), BF16)
    send_ref[far ^ 1] = jnp.zeros((SHARD, LANES), BF16)

    cross_grads = [gradients(task) for task in tasks[4:6]]
    query_sum = 0.5 * repeat_rows(query_sum, 2, scr) + jnp.concatenate([part[0] for part in cross_grads], axis=0)
    repeat_rows(query_sum, 2, scr)
    repeat_rows(jnp.concatenate([cross_grads[1][1].T, cross_grads[0][1].T], axis=0), 2, scr2)
    for half in range(2):
        total = None
        for task in tasks[2 * half : 2 * half + 2]:
            query_part, key_part = gradients(task)
            span = slice(task[1], task[1] + 256)
            query_part = SCALE * (query_part + 0.5 * scr[span, :])
            front_ref[span, :] = jnp.where(low_lanes(256), front_ref[span, :], query_part.astype(BF16))
            total = key_part if total is None else total + key_part
        span = slice(512 * half, 512 * (half + 1))
        local_ref[span, :] = total.T + 0.5 * scr2[span, :]


def far_grads_kernel(
    place_ref, got_ref, got4_ref, grad2_ref, grad3_ref, own_ref, beside_ref, across_ref, opposite_ref, sums, scr
):
    second, upper, far = place_ref[0], place_ref[1], place_ref[2]
    total = None
    for level in reversed(range(5, LEVELS)):
        count = 2 ** (level - 4)
        base = (far ^ count) & (16 - count)
        part = BLOCK // count
        here = got_ref[base, 0:part, :].astype(F32)
        for child in range(1, count):
            here = here + got_ref[base + child, 0:part, :].astype(F32)
        total = here if total is None else here + 0.5 * repeat_rows(total, 2, scr)
    total = got4_ref[...].astype(F32) + 0.5 * repeat_rows(total, 2, scr)
    sums[...] = total.reshape(4, BLOCK // 4, LANES)
    own = 2 * upper + second
    across_ref[...] = (0.5 * repeat_rows(sums[own ^ 2], 2, scr) + grad3_ref[second]).astype(BF16)
    opposite_ref[...] = 0.5 * repeat_rows(sums[own ^ 3], 2, scr) + grad3_ref[1 - second]
    beside_ref[...] = (0.25 * repeat_rows(sums[own ^ 1], 4, scr) + grad2_ref[...]).astype(BF16)
    own_ref[...] = 0.25 * repeat_rows(sums[own], 4, scr)


def relay_kernel(own_ref, got_ref, out_ref):
    out_ref[...] = (own_ref[...] + got_ref[...].astype(F32)).astype(BF16)


def own_grads_kernel(beside_ref, opposite_ref, kept_ref, local_ref, front_ref, out_ref, scr):
    total = kept_ref[...] + beside_ref[...].astype(F32)
    total = total + 0.5 * repeat_rows(opposite_ref[...].astype(F32), 2, scr)
    repeat_rows(total, 4, scr)
    for head in range(HEADS):
        span = slice(head * SHARD, (head + 1) * SHARD)
        out_ref[head, :, 0:LANES] = front_ref[span, :]
        out_ref[head, :, LANES : 2 * LANES] = (local_ref[span, :] + 0.25 * scr[span, :]).astype(BF16)


def call(kernel, outs, scratch, megabytes, in_specs):
    return pl.pallas_call(
        kernel,
        out_shape=outs,
        in_specs=in_specs,
        out_specs=jax.tree.map(lambda _: VMEM, outs),
        scratch_shapes=scratch,
        compiler_params=pltpu.CompilerParams(vmem_limit_bytes=megabytes * 2**20),
    )


def wide(rows):
    return pltpu.VMEM((rows + 8, LANES), F32)


def on_device(far_groups, head_groups, queries, key_tokens, value_tokens, cotangent):
    seq_place, grp_place = lax.axis_index("seq"), lax.axis_index("grp")
    far_place = (seq_place >> 5 & 3) | grp_place << 2
    place = jnp.stack([seq_place >> 3 & 1, seq_place >> 4 & 1, far_place]).astype(jnp.int32)
    block, block32 = shape((BLOCK, LANES), BF16), shape((BLOCK, LANES), F32)
    packed_shape = shape((HEADS, SHARD, 2 * LANES), BF16)

    def exchange(slots, groups):
        return lax.all_to_all(slots, ("grp", "seq"), 0, 0, axis_index_groups=groups)

    def swap(rows, mask):
        return lax.ppermute(rows, "seq", [(source, source ^ mask) for source in range(lax.axis_size("seq"))])

    packed = call(
        pack_kernel,
        packed_shape,
        [pltpu.VMEM((SHARD, HEADS * HEAD_DIM), BF16)] * 4 + [pltpu.SemaphoreType.DMA((4,))],
        60,
        [pl.BlockSpec(memory_space=pl.ANY)] * 4,
    )(queries, key_tokens, value_tokens, cotangent)
    own = exchange(packed, head_groups).reshape(ROWS, 2 * LANES)
    half = shape((SHARD, LANES), BF16)
    level1, level2, level3 = call(
        pool_own_kernel, (shape((512, LANES), BF16), block, half), [wide(ROWS)], 8, [VMEM]
    )(own)
    opposite = swap(level3, 24)
    sib2 = swap(level2, 8)
    across = swap(opposite, 8)
    sib3, level4, slots = call(
        region_kernel, (block, block, shape((16, SHARD, LANES), BF16)), [wide(BLOCK)], 8, [SMEM] + [VMEM] * 4
    )(place, level3, sib2, opposite, across)
    sib4 = swap(level4, 32)
    far_rows = exchange(slots, far_groups)
    upper_rows = TOTAL_ROWS - STARTS[2]
    front, local, grad2, grad3, grad4, slots = call(
        main_kernel,
        (
            shape((ROWS, LANES), BF16),
            shape((ROWS, LANES), F32),
            block32,
            shape((2, SHARD, LANES), F32),
            block,
            shape((16, SHARD, LANES), BF16),
        ),
        [
            pltpu.VMEM((TOTAL_ROWS, LANES), BF16),
            pltpu.VMEM((TOTAL_ROWS, LANES), BF16),
            pltpu.VMEM((4, 256, 512), BF16),
            pltpu.VMEM((2, 256, 256), BF16),
            pltpu.VMEM((upper_rows, 256), BF16),
            wide(TOTAL_ROWS),
            wide(TOTAL_ROWS),
            wide(TOTAL_ROWS),
            wide(TOTAL_ROWS),
            pltpu.VMEM((3, BLOCK, LANES), BF16),
            wide(ROWS),
            wide(ROWS),
        ],
        32,
        [SMEM] + [VMEM] * 6,
    )(place, own, level1, sib2, sib3, sib4, far_rows)
    got4 = swap(grad4, 32)
    kept, beside, across, opposite = call(
        far_grads_kernel,
        (block32, block, half, shape((SHARD, LANES), F32)),
        [pltpu.VMEM((4, BLOCK // 4, LANES), F32), wide(BLOCK)],
        8,
        [SMEM] + [VMEM] * 4,
    )(place, exchange(slots, far_groups), got4, grad2, grad3)
    relayed = call(relay_kernel, half, [], 8, [VMEM] * 2)(opposite, swap(across, 8))
    packed = call(own_grads_kernel, packed_shape, [wide(ROWS)], 8, [VMEM] * 5)(
        swap(beside, 8), swap(relayed, 24), kept, local, front
    )
    return pl.pallas_call(
        unpack_kernel,
        out_shape=(shape((SHARD, HEADS * HEAD_DIM), BF16),) * 4,
        in_specs=[VMEM],
        out_specs=(pl.BlockSpec(memory_space=pl.ANY),) * 4,
        scratch_shapes=[pltpu.VMEM((SHARD, HEADS * HEAD_DIM), BF16)] * 4 + [pltpu.SemaphoreType.DMA((4,))],
        compiler_params=pltpu.CompilerParams(vmem_limit_bytes=8 * 2**20),
    )(exchange(packed, head_groups))


def groups_over(bits, devices):
    mask = sum(1 << bit for bit in bits)
    offsets = [sum((number >> order & 1) << bit for order, bit in enumerate(bits)) for number in range(2 ** len(bits))]
    return [[base + offset for offset in offsets] for base in range(devices) if base & mask == 0]


def solution(mesh):
    devices = mesh.size
    spec = P(("grp", "seq"), None)
    return jax.shard_map(
        functools.partial(
            on_device,
            groups_over((5, 6, 7, 8), devices),
            groups_over((0, 1, 2), devices),
        ),
        mesh=mesh,
        in_specs=(spec,) * 4,
        out_specs=(spec,) * 4,
        check_vma=False,
    )
```
